128 devices in a mesh: gx: 16 (over z, x), gy: 8 (over y, core).
Axes of the slice: x: 4, y: 4, z: 4, core: 2. Of those that a mesh axis runs over, the one named last changes fastest.
Arguments:
- right_side: float32 [16384, 128], P(('gx', 'gy'))
- compress: float32 [16384, 128], P(('gx', 'gy')), may hold values from 0.5 to 8
- block_fill: int32 [16384], P(('gx', 'gy')), may hold values from 32 to 128, as said below
- pair_home: int32 [49152], P(('gx', 'gy')), may hold values from 0 to 16383, as said below
- pair_far: int32 [49152], P(('gx', 'gy')), may hold values from 0 to 16383, as said below
- pair_count: int32 [128], P(('gx', 'gy')), may hold values from 1 to 384, as said below
- weights: bfloat16 [49152, 128, 128], P(('gx', 'gy')), may hold values from 0 to 0.015625
Outputs:
- solution_field: float32 [16384, 128], P(('gx', 'gy'))
- residual: float32 [16384, 128], P(('gx', 'gy'))
The draws below stay inside these ranges and needn't reach their ends.
Inputs may be any that keep to these rules, and one draw needn't show every extreme that they name: `pair_home`: pair slot s names as first block a block of device s // 384, blocks of device d being d * 128 to d * 128 + 127, devices numbered gx major. `pair_far`: the second block belongs to the slot's device or to one of its eight neighbours on the periodic gx by gy grid of devices. `pair_count`: slots after a device's count are ignored; some devices hold 384. `block_fill`: slots after a block's fill are padding; some block holds 128.
All inputs are finite; a program needn't handle non-finite values.
Results may differ from the reference program's by a relative error of at most 0.015.
Values may be sent and summed in bfloat16 or wider, within the bound.
No kernel may reach another device: no remote copies, remote signals or barrier semaphores. Data moves between devices by JAX's collectives and lax.ppermute only.
A program may use at most 64 MiB of HBM per device.

```python
import math
import jax
import jax.numpy as jnp
from jax import lax

TILE = 128
BLK_DEV = 128
PAIRS_DEV = 384
ITERS = 3
NBLK = 16384
NPAIR = 49152
N_GX = 16
N_GY = 8
DEVICES = 128


def draw_right_side(key, part):
    ramp = 1.0 + 2.0 * jnp.arange(NBLK, dtype=jnp.float32)[:, None] / max(NBLK - 1, 1)
    rough = jax.random.normal(key, (NBLK, TILE), jnp.float32)
    return jnp.clip(rough, -4.0, 4.0) * ramp


def draw_block_fill(key, part):
    fill = jax.random.randint(jax.random.fold_in(key, 11), (NBLK,), TILE // 4, TILE + 1)
    where = jax.random.randint(jax.random.fold_in(key, 12), (), 0, NBLK)
    return fill.at[where].set(TILE).astype(jnp.int32)


def draw_pair_home(key, part):
    device = jnp.arange(NPAIR, dtype=jnp.int32) // PAIRS_DEV
    inside = jax.random.randint(jax.random.fold_in(key, 21), (NPAIR,), 0, BLK_DEV)
    return (device * BLK_DEV + inside).astype(jnp.int32)


def draw_pair_far(key, part):
    device = jnp.arange(NPAIR, dtype=jnp.int32) // PAIRS_DEV
    first_index = device // N_GY
    second_index = device % N_GY
    step_first = jax.random.randint(jax.random.fold_in(key, 31), (NPAIR,), -1, 2)
    step_second = jax.random.randint(jax.random.fold_in(key, 32), (NPAIR,), -1, 2)
    target = (first_index + step_first) % N_GX * N_GY + (second_index + step_second) % N_GY
    inside = jax.random.randint(jax.random.fold_in(key, 33), (NPAIR,), 0, BLK_DEV)
    return (target * BLK_DEV + inside).astype(jnp.int32)


def draw_pair_count(key, part):
    device = jnp.arange(DEVICES, dtype=jnp.int32)
    band = jax.random.randint(jax.random.fold_in(key, 41), (), 0, N_GX)
    heavy = (device // N_GY - band) % N_GX < 2
    light = jax.random.randint(jax.random.fold_in(key, 42), (DEVICES,), PAIRS_DEV // 8, PAIRS_DEV // 3 + 1)
    return jnp.where(heavy, PAIRS_DEV, light).astype(jnp.int32)


def steps_of(key, shape, split, smallest, largest):
    def one(position, blocks):
        draws = jax.random.uniform(jax.random.fold_in(jax.random.fold_in(key, 6), position), (blocks,), jnp.float32, smallest / len(split), largest / len(split))
        return jnp.repeat(jnp.exp(draws), shape[position] // blocks).reshape((-1,) + (1,) * (len(shape) - position - 1))

    loudness = one(*split[0])
    for cut in split[1:]:
        loudness = loudness * one(*cut)
    return loudness


def setup_inputs(seed: int = 0) -> dict:
    keys = jax.random.split(jax.random.key(seed), 8)
    return {
        "right_side": draw_right_side(jax.random.fold_in(keys[7], 71), 0),
        "compress": jnp.clip(jnp.exp(math.log(8.0) - 2.7725887 * jax.random.uniform(keys[1], (NBLK, TILE), jnp.float32) ** steps_of(keys[1], (NBLK, TILE), ((0, 128),), -0.2, 0.2)), 0.5, 8.0),
        "block_fill": draw_block_fill(jax.random.fold_in(keys[7], 71), 0),
        "pair_home": draw_pair_home(jax.random.fold_in(keys[7], 71), 0),
        "pair_far": draw_pair_far(jax.random.fold_in(keys[7], 71), 0),
        "pair_count": draw_pair_count(jax.random.fold_in(keys[7], 71), 0),
        "weights": jnp.clip(0.015625 * jax.random.uniform(keys[6], (NPAIR, TILE, TILE), jnp.float32) ** steps_of(keys[6], (NPAIR, TILE, TILE), ((0, 128),), -0.2, 0.2), 0.0, 0.015625).astype(jnp.bfloat16),
    }


def apply_operator(field, compress, live, weights, pair_home, pair_far, slot_live):
    quant = (live * field).astype(jnp.bfloat16).astype(jnp.float32)
    stacks = (weights.reshape(DEVICES, PAIRS_DEV, TILE, TILE), pair_home.reshape(DEVICES, PAIRS_DEV),
              pair_far.reshape(DEVICES, PAIRS_DEV), slot_live.reshape(DEVICES, PAIRS_DEV))

    def one_device(totals, pieces):
        tiles, homes, fars, keep = pieces
        tiles = tiles.astype(jnp.float32)
        row_sum = jnp.sum(tiles, axis=2)
        col_sum = jnp.sum(tiles, axis=1)
        first = quant[homes]
        second = quant[fars]
        toward = jnp.einsum("pij,pj->pi", tiles, second, precision=lax.Precision.HIGHEST)
        backward = jnp.einsum("pij,pi->pj", tiles, first, precision=lax.Precision.HIGHEST)
        term_home = (row_sum * first - toward) * keep[:, None]
        term_far = (col_sum * second - backward) * keep[:, None]
        totals = totals.at[homes].add(term_home).at[fars].add(term_far)
        return totals, None

    pairs_sum, _ = lax.scan(one_device, jnp.zeros((NBLK, TILE), jnp.float32), stacks)
    return compress * field + live * pairs_sum


def reference(right_side, compress, block_fill, pair_home, pair_far, pair_count, weights):
    live = (jnp.arange(TILE, dtype=jnp.int32)[None, :] < block_fill[:, None]).astype(jnp.float32)
    slot_index = jnp.arange(NPAIR, dtype=jnp.int32)
    slot_live = ((slot_index % PAIRS_DEV) < pair_count[slot_index // PAIRS_DEV]).astype(jnp.float32)
    solution_field = jnp.zeros_like(right_side)
    residual = right_side
    direction = right_side
    norm_now = jnp.sum(residual * residual)
    for step in range(ITERS):
        image = apply_operator(direction, compress, live, weights, pair_home, pair_far, slot_live)
        alpha = norm_now / jnp.sum(direction * image)
        solution_field = solution_field + alpha * direction
        residual = residual - alpha * image
        norm_next = jnp.sum(residual * residual)
        direction = residual + (norm_next / norm_now) * direction
        norm_now = norm_next
    return solution_field, residual
```

```python
import jax
import jax.numpy as jnp
from jax import lax
from jax.experimental import pallas as pl
from jax.experimental.pallas import tpu as pltpu
from jax.sharding import PartitionSpec as P

SHIFT = 4.0
COMPRESS_MIN = 0.5
GROUP = 16
CHUNKS = 3
F32 = jnp.float32
BF16 = jnp.bfloat16
BOTH = ("gx", "gy")


def dot_rows(a, b):
    return lax.dot_general(a, b, (((1,), (0,)), ((), ())), preferred_element_type=F32)


def dot_cols(a, b):
    return lax.dot_general(a, b, (((1,), (1,)), ((), ())), preferred_element_type=F32)


def split(x):
    high = x.astype(BF16)
    return high, (x - high.astype(F32)).astype(BF16)


def placed(onehot, terms):
    both = dot_rows(onehot, jnp.concatenate(split(terms), axis=1))
    return both[:, :128] + both[:, 128:]


def pair_products(with_sums, weights, far_q, home_q, toward, backward, row_sum, col_sum):
    npairs = weights.shape[0]
    per_chunk = npairs // GROUP // CHUNKS
    sublane = lax.broadcasted_iota(jnp.int32, (8, 128), 0)
    zero = jnp.zeros((8, 128), F32)

    def group(base):
        rows = pl.ds(base, GROUP)
        far, home = far_q[rows, :], home_q[rows, :]
        if with_sums:
            ones = jnp.ones((GROUP, 128), BF16)
            far, home = jnp.concatenate([far, ones]), jnp.concatenate([home, ones])
        results = [[zero, zero] for _ in range(4)]
        for pair in range(0, GROUP, 2):
            first, second = weights[base + pair], weights[base + pair + 1]
            to = dot_cols(far, jnp.concatenate([first, second], axis=0))
            back = dot_rows(home, jnp.concatenate([first, second], axis=1))
            for which in range(2):
                slot = pair + which
                half, here = slot // 8, sublane == slot % 8
                columns = slice(128 * which, 128 * which + 128)
                for index, product in ((0, to), (1, back)):
                    for offset in (0, GROUP) if with_sums else (0,):
                        got = product[offset + 8 * half : offset + 8 * half + 8, columns]
                        kind = index + (2 if offset else 0)
                        results[kind][half] = jnp.where(here, got, results[kind][half])
        outputs = (toward, backward, row_sum, col_sum) if with_sums else (toward, backward)
        for out, result in zip(outputs, results):
            out[rows, :] = jnp.concatenate(result)

    def chunk(index, carry):
        for inner in range(per_chunk):
            group(pl.multiple_of((index * per_chunk + inner) * GROUP, GROUP))
        return carry

    lax.fori_loop(0, CHUNKS, chunk, 0)


def gathered(near, pick_far, pick_home, far_q, home_q):
    blocks = near.shape[0] // 9
    far_q[...] = dot_rows(pick_far[...], near[...]).astype(BF16)
    home_q[...] = dot_rows(pick_home[...], near[4 * blocks : 5 * blocks, :]).astype(BF16)


def first_kernel(weights, near, pick_far, pick_home, put_far, put_home,
                 own, own_diag, away, far_q, home_q, toward, backward, row_sum, col_sum):
    blocks = own.shape[0]
    centre = slice(4 * blocks, 5 * blocks)
    gathered(near, pick_far, pick_home, far_q, home_q)
    pair_products(True, weights, far_q, home_q, toward, backward, row_sum, col_sum)
    far_terms = placed(put_far[...], backward[...])
    far_diag = placed(put_far[...], col_sum[...])
    own[...] = placed(put_home[...], toward[...]) + far_terms[centre]
    own_diag[...] = placed(put_home[...], row_sum[...]) + far_diag[centre]
    high, low = split(far_diag)
    for slot in range(9):
        rows = slice(slot * blocks, slot * blocks + blocks)
        away[slot, 0] = far_terms[rows].astype(BF16)
        away[slot, 1] = high[rows]
        away[slot, 2] = low[rows]


def middle_kernel(weights, near, pick_far, pick_home, put_far, put_home,
                  own, away, far_q, home_q, toward, backward):
    blocks = own.shape[0]
    gathered(near, pick_far, pick_home, far_q, home_q)
    pair_products(False, weights, far_q, home_q, toward, backward, None, None)
    far_terms = placed(put_far[...], backward[...])
    own[...] = placed(put_home[...], toward[...]) + far_terms[4 * blocks : 5 * blocks]
    for slot in range(9):
        away[slot] = far_terms[slot * blocks : slot * blocks + blocks].astype(BF16)


def last_kernel(weights, near, pick_far, pick_home, put_far, put_home, v0, v1, v2, diag,
                own, away, dots, far_q, home_q, toward, backward):
    blocks = own.shape[0]
    gathered(near, pick_far, pick_home, far_q, home_q)
    pair_products(False, weights, far_q, home_q, toward, backward, None, None)
    far_terms = placed(put_far[...], backward[...])
    home_terms = placed(put_home[...], toward[...])
    own[...] = home_terms + far_terms[4 * blocks : 5 * blocks]
    for slot in range(9):
        away[slot] = far_terms[slot * blocks : slot * blocks + blocks].astype(BF16)
    a, b, c = v0[...], v1[...], v2[...]
    quant = near[4 * blocks : 5 * blocks, :].astype(F32)
    energy = diag[...] * c * c - 2.0 * quant * home_terms
    lane = lax.broadcasted_iota(jnp.int32, (1, 128), 1)
    row = jnp.zeros((1, 128), F32)
    for index, product in enumerate((a * a, a * b, a * c, b * b, b * c, c * c, energy)):
        total = jnp.sum(jnp.sum(product, axis=0, keepdims=True), axis=1, keepdims=True)
        row = jnp.where(lane == index, total, row)
    dots[...] = jnp.broadcast_to(row, dots.shape)


def finish_kernel(dots, v0, v1, v2, a2, solution_field, residual):
    row = jnp.sum(dots[...], axis=0, keepdims=True)
    lane = lax.broadcasted_iota(jnp.int32, row.shape, 1)

    def entry(index):
        return jnp.sum(jnp.where(lane == index, row, 0.0), axis=1, keepdims=True)

    g00, g01, g02, g11, g12, g22, m22 = (entry(index) for index in range(7))
    gram = ((g00, g01, g02), (g01, g11, g12), (g02, g12, g22))
    m00 = g01 + SHIFT * g00
    m01 = g11 + SHIFT * g01
    m11 = g12 + SHIFT * g11
    m02 = g12 + SHIFT * g02
    m12 = g22 + SHIFT * g12
    energies = ((m00, m01, m02), (m01, m11, m12), (m02, m12, m22))

    def form(matrix, p):
        return sum(p[i] * p[j] * matrix[i][j] for i in range(len(p)) for j in range(len(p)))

    def step_size(norm, p):
        floor = jnp.maximum(COMPRESS_MIN * norm, 1e-30)
        return norm / jnp.maximum(form(energies, p), floor)

    def moved(r, alpha, p):
        image = [SHIFT * p[i] + (p[i - 1] if i else 0.0) for i in range(len(p))] + [p[-1]]
        return [(r[i] if i < len(r) else 0.0) - alpha * image[i] for i in range(len(image))]

    def turned(r, beta, p):
        return [r[i] + beta * p[i] if i < len(p) else r[i] for i in range(len(r))]

    def norm_of(r):
        return jnp.maximum(form(gram, r), 0.0)

    one = jnp.ones_like(g00)
    p0 = [one]
    alpha0 = step_size(g00, p0)
    r1 = moved([one], alpha0, p0)
    n1 = norm_of(r1)
    p1 = turned(r1, n1 / jnp.maximum(g00, 1e-30), p0)
    alpha1 = step_size(n1, p1)
    r2 = moved(r1, alpha1, p1)
    n2 = norm_of(r2)
    p2 = turned(r2, n2 / jnp.maximum(n1, 1e-30), p1)
    alpha2 = step_size(n2, p2)
    x = [alpha0 * p0[0] + alpha1 * p1[0] + alpha2 * p2[0], alpha1 * p1[1] + alpha2 * p2[1], alpha2 * p2[2]]
    images = [SHIFT * p2[0], p2[0] + SHIFT * p2[1], p2[1]]
    r = [r2[i] - alpha2 * images[i] for i in range(3)]
    a, b, c = v0[...], v1[...], v2[...]
    solution_field[...] = x[0] * a + x[1] * b + x[2] * c
    residual[...] = r[0] * a + r[1] * b + r[2] * c - (alpha2 * p2[2]) * a2[...]


def shifted(value, axis, step):
    count = lax.axis_size(axis)
    return lax.ppermute(value, axis, [(source, (source + step) % count) for source in range(count)])


def neighbours(quant):
    mine = quant[None]
    column = jnp.concatenate([shifted(mine, "gx", 1), mine, shifted(mine, "gx", -1)])
    return jnp.concatenate([shifted(column, "gy", 1), column, shifted(column, "gy", -1)])


def returned(own, away):
    parts = away.reshape(3, 3, *own.shape)
    low, high = shifted(parts[2], "gy", 1), shifted(parts[0], "gy", -1)
    column = parts[1].astype(F32) + low.astype(F32) + high.astype(F32)
    mine = own + low[1].astype(F32) + high[1].astype(F32)
    low, high = shifted(column[2].astype(BF16), "gx", 1), shifted(column[0].astype(BF16), "gx", -1)
    return mine + low.astype(F32) + high.astype(F32)


def returned_with_diag(own, own_diag, away):
    parts = away.reshape(3, 3, 3, *own.shape)
    low, high = shifted(parts[2], "gy", 1), shifted(parts[0], "gy", -1)

    def terms(x, a):
        return x[a, 0].astype(F32)

    def diags(x, a):
        return x[a, 1].astype(F32) + x[a, 2].astype(F32)

    def packed(a):
        total = terms(parts[1], a) + terms(low, a) + terms(high, a)
        diag = diags(parts[1], a) + diags(low, a) + diags(high, a)
        return jnp.stack([total.astype(BF16), *split(diag)])[None]

    up, down = packed(2), packed(0)
    mine = own + terms(low, 1) + terms(high, 1)
    mine_diag = own_diag + diags(low, 1) + diags(high, 1)
    low, high = shifted(up, "gx", 1), shifted(down, "gx", -1)
    return mine + terms(low, 0) + terms(high, 0), mine_diag + diags(low, 0) + diags(high, 0)


def call(kernel, outs, scratch, args):
    vmem = pl.BlockSpec(memory_space=pltpu.VMEM)
    return pl.pallas_call(
        kernel,
        out_shape=outs,
        in_specs=[vmem] * len(args),
        out_specs=[vmem] * len(outs),
        scratch_shapes=scratch,
        compiler_params=pltpu.CompilerParams(vmem_limit_bytes=30 * 2**20),
    )(*args)


def on_device(right_side, compress, block_fill, pair_home, pair_far, pair_count, weights):
    blocks, tile = right_side.shape
    npairs = weights.shape[0]
    size_first, size_second = lax.axis_size("gx"), lax.axis_size("gy")
    first_index, second_index = lax.axis_index("gx"), lax.axis_index("gy")
    my_device = first_index * size_second + second_index
    live = (jnp.arange(tile, dtype=jnp.int32)[None, :] < block_fill[:, None]).astype(F32)

    def near_of(vector):
        return neighbours((live * vector).astype(BF16)).reshape(9 * blocks, tile)

    near0 = near_of(right_side)

    kept = jnp.arange(npairs, dtype=jnp.int32) < pair_count[0]
    far_device = pair_far // blocks
    slot_first = (far_device // size_second - first_index + 1) % size_first
    slot_second = (far_device % size_second - second_index + 1) % size_second
    far = (slot_second * 3 + slot_first) * blocks + pair_far % blocks
    far = jnp.where(kept, far, -1)
    home = jnp.where(kept, pair_home - my_device * blocks, -1)

    def onehots(index, count):
        choices = jnp.arange(count, dtype=jnp.int32)
        return (
            (index[:, None] == choices[None, :]).astype(BF16),
            (choices[:, None] == index[None, :]).astype(BF16),
        )

    pick_far, put_far = onehots(far, 9 * blocks)
    pick_home, put_home = onehots(home, blocks)
    weights = pltpu.with_memory_space_constraint(weights, pltpu.VMEM)
    routes = (pick_far, pick_home, put_far, put_home)

    def shape(*dims, dtype=F32):
        return jax.ShapeDtypeStruct(dims, dtype)

    own_shape = shape(blocks, tile)
    away_shape = shape(9, blocks, tile, dtype=BF16)
    rows16, rows32 = pltpu.VMEM((npairs, tile), BF16), pltpu.VMEM((npairs, tile), F32)

    own, own_diag, away = call(
        first_kernel,
        [own_shape, own_shape, shape(9, 3, blocks, tile, dtype=BF16)],
        [rows16, rows16, rows32, rows32, rows32, rows32],
        (weights, near0, *routes),
    )
    total, pair_diag = returned_with_diag(own, own_diag, away)
    diag = compress + live * pair_diag
    v0 = right_side
    v1 = (diag - SHIFT) * v0 - live * total

    own, away = call(
        middle_kernel,
        [own_shape, away_shape],
        [rows16, rows16, rows32, rows32],
        (weights, near_of(v1), *routes),
    )
    v2 = (diag - SHIFT) * v1 - live * returned(own, away)

    own, away, dots = call(
        last_kernel,
        [own_shape, away_shape, shape(128, tile)],
        [rows16, rows16, rows32, rows32],
        (weights, near_of(v2), *routes, v0, v1, v2, diag),
    )
    a2 = diag * v2 - live * returned(own, away)
    dots = lax.all_to_all(dots, BOTH, 0, 0, tiled=True)
    return tuple(call(finish_kernel, [own_shape, own_shape], [], (dots, v0, v1, v2, a2)))


def solution(mesh):
    return jax.shard_map(
        on_device,
        mesh=mesh,
        in_specs=(
            P(BOTH, None),
            P(BOTH, None),
            P(BOTH),
            P(BOTH),
            P(BOTH),
            P(BOTH),
            P(BOTH, None, None),
        ),
        out_specs=(P(BOTH, None), P(BOTH, None)),
        check_vma=False,
    )
```

```python
import functools

import jax
import jax.numpy as jnp
from jax import lax
from jax.experimental import pallas as pl
from jax.experimental.pallas import tpu as pltpu
from jax.sharding import PartitionSpec as P

SHIFT = 4.0
COMPRESS_MIN = 0.5
GROUP = 16
F32 = jnp.float32
BF16 = jnp.bfloat16
BOTH = ("gx", "gy")


def dot_rows(a, b):
    return lax.dot_general(a, b, (((1,), (0,)), ((), ())), preferred_element_type=F32)


def dot_cols(a, b):
    return lax.dot_general(a, b, (((1,), (1,)), ((), ())), preferred_element_type=F32)


def placed(onehot, terms):
    high = terms.astype(BF16)
    low = (terms - high.astype(F32)).astype(BF16)
    both = dot_rows(onehot, jnp.concatenate([high, low], axis=1))
    return both[:, :128] + both[:, 128:]


def pair_products(weights, vectors, out, sums, across, chunks, arrive=None):
    per_chunk = weights.shape[0] // GROUP // chunks
    sublane = lax.broadcasted_iota(jnp.int32, (8, 128), 0)
    zero = jnp.zeros((8, 128), F32)

    def group(base):
        rows = pl.ds(base, GROUP)
        left = vectors[rows, :]
        if sums is not None:
            left = jnp.concatenate([left, jnp.ones((GROUP, 128), BF16)])
        results = [[zero, zero], [zero, zero]]
        for pair in range(0, GROUP, 2):
            first, second = weights[base + pair], weights[base + pair + 1]
            if across:
                product = dot_cols(left, jnp.concatenate([first, second], axis=0))
            else:
                product = dot_rows(left, jnp.concatenate([first, second], axis=1))
            for which in range(2):
                half, here = (pair + which) // 8, sublane == (pair + which) % 8
                columns = slice(128 * which, 128 * which + 128)
                for kind in range(1 if sums is None else 2):
                    start = GROUP * kind + 8 * half
                    results[kind][half] = jnp.where(here, product[start : start + 8, columns], results[kind][half])
        out[rows, :] = jnp.concatenate(results[0])
        if sums is not None:
            sums[rows, :] = jnp.concatenate(results[1])

    def chunk(index, carry):
        if arrive is not None:
            arrive(index)
        for inner in range(per_chunk):
            group(pl.multiple_of((index * per_chunk + inner) * GROUP, GROUP))
        return carry

    lax.fori_loop(0, chunks, chunk, 0)


def send_terms(terms, up, down, middle, first):
    blocks = up.shape[1]
    for second in range(3):
        for target, slot in ((down, 0), (up, 2)):
            row = (3 * second + slot) * blocks
            target[first + second] = terms[row : row + blocks].astype(BF16)
        row = (3 * second + 1) * blocks
        middle[second] = terms[row : row + blocks]


def start_kernel(chunks, weights, quant, pick_home, put_far,
                 held, up, down, middle, middle_diag, vectors, products, sums, arrived):
    per_chunk = weights.shape[0] // chunks

    def copy(index):
        part = pl.ds(index * per_chunk, per_chunk)
        return pltpu.make_async_copy(weights.at[part], held.at[part], arrived.at[index])

    for index in range(chunks):
        copy(index).start()
    q = quant[...]
    up[0] = q
    down[0] = q
    vectors[...] = dot_rows(pick_home[...], q).astype(BF16)
    pair_products(held, vectors, products, sums, False, chunks, lambda index: copy(index).wait())
    send_terms(placed(put_far[...], products[...]), up, down, middle, 1)
    send_terms(placed(put_far[...], sums[...]), up, down, middle_diag, 4)


def toward_home(weights, near, pick_far, put_home, vectors, products, sums):
    vectors[...] = dot_rows(pick_far[...], near[...]).astype(BF16)
    pair_products(weights, vectors, products, sums, True, 3)
    return placed(put_home[...], products[...])


def away_next(weights, v, live, pick_home, put_far, up, down, middle, vectors, products):
    q = (live * v).astype(BF16)
    up[0] = q
    down[0] = q
    vectors[...] = dot_rows(pick_home[...], q).astype(BF16)
    pair_products(weights, vectors, products, None, False, 3)
    send_terms(placed(put_far[...], products[...]), up, down, middle, 1)


def second_kernel(weights, near, pick_far, put_home, pick_home, put_far, far_total, far_diag, v, live, compress,
                  after, diag_out, up, down, middle, vectors, products, sums):
    total = toward_home(weights, near, pick_far, put_home, vectors, products, sums) + far_total[...]
    mask = live[...]
    diag = compress[...] + mask * (placed(put_home[...], sums[...]) + far_diag[...])
    diag_out[...] = diag
    result = (diag - SHIFT) * v[...] - mask * total
    after[...] = result
    away_next(weights, result, mask, pick_home, put_far, up, down, middle, vectors, products)


def third_kernel(weights, near, pick_far, put_home, pick_home, put_far, far_total, v, live, diag,
                 after, up, down, middle, vectors, products):
    total = toward_home(weights, near, pick_far, put_home, vectors, products, None) + far_total[...]
    mask = live[...]
    result = (diag[...] - SHIFT) * v[...] - mask * total
    after[...] = result
    away_next(weights, result, mask, pick_home, put_far, up, down, middle, vectors, products)


def image_kernel(weights, near, pick_far, put_home, far_total, v, live, diag, after, vectors, products):
    total = toward_home(weights, near, pick_far, put_home, vectors, products, None) + far_total[...]
    after[...] = diag[...] * v[...] - live[...] * total


def dots_kernel(v0, v1, v2, diag, live, far_total, dots):
    a, b, c = v0[...], v1[...], v2[...]
    energy = diag[...] * c * c - 2.0 * (live[...] * c) * far_total[...]
    lane = lax.broadcasted_iota(jnp.int32, (1, 128), 1)
    row = jnp.zeros((1, 128), F32)
    for index, product in enumerate((a * a, a * b, a * c, b * b, b * c, c * c, energy)):
        total = jnp.sum(jnp.sum(product, axis=0, keepdims=True), axis=1, keepdims=True)
        row = jnp.where(lane == index, total, row)
    dots[...] = jnp.broadcast_to(row, dots.shape)


def finish_kernel(dots, v0, v1, v2, a2, solution_field, residual):
    row = jnp.sum(dots[...], axis=0, keepdims=True)
    lane = lax.broadcasted_iota(jnp.int32, row.shape, 1)

    def entry(index):
        return jnp.sum(jnp.where(lane == index, row, 0.0), axis=1, keepdims=True)

    g00, g01, g02, g11, g12, g22, m22 = (entry(index) for index in range(7))
    gram = ((g00, g01, g02), (g01, g11, g12), (g02, g12, g22))
    m00 = g01 + SHIFT * g00
    m01 = g11 + SHIFT * g01
    m11 = g12 + SHIFT * g11
    m02 = g12 + SHIFT * g02
    m12 = g22 + SHIFT * g12
    energies = ((m00, m01, m02), (m01, m11, m12), (m02, m12, m22))

    def form(matrix, p):
        return sum(p[i] * p[j] * matrix[i][j] for i in range(len(p)) for j in range(len(p)))

    def step_size(norm, p):
        floor = jnp.maximum(COMPRESS_MIN * norm, 1e-30)
        return norm / jnp.maximum(form(energies, p), floor)

    def moved(r, alpha, p):
        image = [SHIFT * p[i] + (p[i - 1] if i else 0.0) for i in range(len(p))] + [p[-1]]
        return [(r[i] if i < len(r) else 0.0) - alpha * image[i] for i in range(len(image))]

    def turned(r, beta, p):
        return [r[i] + beta * p[i] if i < len(p) else r[i] for i in range(len(r))]

    def norm_of(r):
        return jnp.maximum(form(gram, r), 0.0)

    one = jnp.ones_like(g00)
    p0 = [one]
    alpha0 = step_size(g00, p0)
    r1 = moved([one], alpha0, p0)
    n1 = norm_of(r1)
    p1 = turned(r1, n1 / jnp.maximum(g00, 1e-30), p0)
    alpha1 = step_size(n1, p1)
    r2 = moved(r1, alpha1, p1)
    n2 = norm_of(r2)
    p2 = turned(r2, n2 / jnp.maximum(n1, 1e-30), p1)
    alpha2 = step_size(n2, p2)
    x = [alpha0 * p0[0] + alpha1 * p1[0] + alpha2 * p2[0], alpha1 * p1[1] + alpha2 * p2[1], alpha2 * p2[2]]
    images = [SHIFT * p2[0], p2[0] + SHIFT * p2[1], p2[1]]
    r = [r2[i] - alpha2 * images[i] for i in range(3)]
    a, b, c = v0[...], v1[...], v2[...]
    solution_field[...] = x[0] * a + x[1] * b + x[2] * c
    residual[...] = r[0] * a + r[1] * b + r[2] * c - (alpha2 * p2[2]) * a2[...]


def shifted(value, axis, step):
    count = lax.axis_size(axis)
    return lax.ppermute(value, axis, [(source, (source + step) % count) for source in range(count)])


def call(kernel, outs, scratch, args, in_hbm=()):
    vmem = pl.BlockSpec(memory_space=pltpu.VMEM)
    return pl.pallas_call(
        kernel,
        out_shape=outs,
        in_specs=[pl.BlockSpec(memory_space=pl.ANY) if i in in_hbm else vmem for i in range(len(args))],
        out_specs=[vmem] * len(outs),
        scratch_shapes=scratch,
        compiler_params=pltpu.CompilerParams(vmem_limit_bytes=36 * 2**20),
    )(*args)


def exchanged(up, down, middle, middle_diag=None):
    low, high = shifted(up, "gx", 1), shifted(down, "gx", -1)
    column = jnp.stack([low[0], up[0], high[0]])

    def summed(second, first, own):
        return own[second] + low[first + second].astype(F32) + high[first + second].astype(F32)

    kinds = [(1, middle)] if middle_diag is None else [(1, middle), (4, middle_diag)]

    def message(second):
        sums = [summed(second, first, own).astype(BF16)[None] for first, own in kinds]
        return jnp.concatenate([column, *sums])

    from_low, from_high = shifted(message(2), "gy", 1), shifted(message(0), "gy", -1)
    near = jnp.concatenate([from_low[:3], column, from_high[:3]])
    near = near.reshape(-1, near.shape[-1])
    totals = [
        summed(1, first, own) + from_low[3 + kind].astype(F32) + from_high[3 + kind].astype(F32)
        for kind, (first, own) in enumerate(kinds)
    ]
    return near, *totals


def on_device(right_side, compress, block_fill, pair_home, pair_far, pair_count, weights):
    blocks, tile = right_side.shape
    npairs = weights.shape[0]
    size_first, size_second = lax.axis_size("gx"), lax.axis_size("gy")
    first_index, second_index = lax.axis_index("gx"), lax.axis_index("gy")
    my_device = first_index * size_second + second_index
    live = (jnp.arange(tile, dtype=jnp.int32)[None, :] < block_fill[:, None]).astype(F32)

    kept = jnp.arange(npairs, dtype=jnp.int32) < pair_count[0]
    far_device = pair_far // blocks
    slot_first = (far_device // size_second - first_index + 1) % size_first
    slot_second = (far_device % size_second - second_index + 1) % size_second
    far = (slot_second * 3 + slot_first) * blocks + pair_far % blocks
    far = jnp.where(kept, far, -1)
    home = jnp.where(kept, pair_home - my_device * blocks, -1)

    def onehots(index, count):
        choices = jnp.arange(count, dtype=jnp.int32)
        return (
            (index[:, None] == choices[None, :]).astype(BF16),
            (choices[:, None] == index[None, :]).astype(BF16),
        )

    pick_far, put_far = onehots(far, 9 * blocks)
    pick_home, put_home = onehots(home, blocks)

    def shape(*dims, dtype=F32):
        return jax.ShapeDtypeStruct(dims, dtype)

    own_shape = shape(blocks, tile)
    middle_shape = shape(3, blocks, tile)
    rows16, rows32 = pltpu.VMEM((npairs, tile), BF16), pltpu.VMEM((npairs, tile), F32)

    def slabs(count):
        return shape(count, blocks, tile, dtype=BF16)

    quant = (live * right_side).astype(BF16)
    chunks = 6
    held, up, down, middle, middle_diag = call(
        functools.partial(start_kernel, chunks),
        [pltpu.VMEM(weights.shape, BF16), slabs(7), slabs(7), middle_shape, middle_shape],
        [rows16, rows32, rows32, pltpu.SemaphoreType.DMA((chunks,))],
        (weights, quant, pick_home, put_far),
        in_hbm=(0,),
    )
    held = pltpu.with_memory_space_constraint(held, pltpu.VMEM)
    near, far_total, far_diag = exchanged(up, down, middle, middle_diag)
    v0 = right_side
    v1, diag, up, down, middle = call(
        second_kernel,
        [own_shape, own_shape, slabs(4), slabs(4), middle_shape],
        [rows16, rows32, rows32],
        (held, near, pick_far, put_home, pick_home, put_far, far_total, far_diag, v0, live, compress),
    )
    near, far_total = exchanged(up, down, middle)
    v2, up, down, middle = call(
        third_kernel,
        [own_shape, slabs(4), slabs(4), middle_shape],
        [rows16, rows32],
        (held, near, pick_far, put_home, pick_home, put_far, far_total, v1, live, diag),
    )
    near, far_total = exchanged(up, down, middle)
    (dots,) = call(dots_kernel, [shape(size_first * size_second, tile)], [], (v0, v1, v2, diag, live, far_total))
    dots = lax.all_to_all(dots, BOTH, 0, 0, tiled=True)
    (image,) = call(
        image_kernel, [own_shape], [rows16, rows32], (held, near, pick_far, put_home, far_total, v2, live, diag)
    )
    return tuple(call(finish_kernel, [own_shape, own_shape], [], (dots, v0, v1, v2, image)))


def solution(mesh):
    return jax.shard_map(
        on_device,
        mesh=mesh,
        in_specs=(
            P(BOTH, None),
            P(BOTH, None),
            P(BOTH),
            P(BOTH),
            P(BOTH),
            P(BOTH),
            P(BOTH, None, None),
        ),
        out_specs=(P(BOTH, None), P(BOTH, None)),
        check_vma=False,
    )
```

```python
import functools

import jax
import jax.numpy as jnp
from jax import lax
from jax.experimental import pallas as pl
from jax.experimental.pallas import tpu as pltpu
from jax.sharding import PartitionSpec as P

SHIFT = 4.0
COMPRESS_MIN = 0.5
GROUP = 16
F32 = jnp.float32
BF16 = jnp.bfloat16
BOTH = ("gx", "gy")


def dot_rows(a, b):
    return lax.dot_general(a, b, (((1,), (0,)), ((), ())), preferred_element_type=F32)


def dot_cols(a, b):
    return lax.dot_general(a, b, (((1,), (1,)), ((), ())), preferred_element_type=F32)


def placed(onehot, terms):
    high = terms.astype(BF16)
    low = (terms - high.astype(F32)).astype(BF16)
    both = dot_rows(onehot, jnp.concatenate([high, low], axis=1))
    return both[:, :128] + both[:, 128:]


def pair_products(weights, vectors, out, sums, across, chunks, arrive=None):
    per_chunk = weights.shape[0] // GROUP // chunks
    sublane = lax.broadcasted_iota(jnp.int32, (8, 128), 0)
    zero = jnp.zeros((8, 128), F32)

    def group(base):
        rows = pl.ds(base, GROUP)
        left = vectors[rows, :]
        if sums is not None:
            left = jnp.concatenate([left, jnp.ones((GROUP, 128), BF16)])
        results = [[zero, zero], [zero, zero]]
        for pair in range(0, GROUP, 2):
            first, second = weights[base + pair], weights[base + pair + 1]
            if across:
                product = dot_cols(left, jnp.concatenate([first, second], axis=0))
            else:
                product = dot_rows(left, jnp.concatenate([first, second], axis=1))
            for which in range(2):
                half, here = (pair + which) // 8, sublane == (pair + which) % 8
                columns = slice(128 * which, 128 * which + 128)
                for kind in range(1 if sums is None else 2):
                    start = GROUP * kind + 8 * half
                    results[kind][half] = jnp.where(here, product[start : start + 8, columns], results[kind][half])
        out[rows, :] = jnp.concatenate(results[0])
        if sums is not None:
            sums[rows, :] = jnp.concatenate(results[1])

    def chunk(index, carry):
        if arrive is not None:
            arrive(index)
        for inner in range(per_chunk):
            group(pl.multiple_of((index * per_chunk + inner) * GROUP, GROUP))
        return carry

    lax.fori_loop(0, chunks, chunk, 0)


def send_terms(terms, up, down, middle, first):
    blocks = up.shape[1]
    for second in range(3):
        for target, slot in ((down, 0), (up, 2)):
            row = (3 * second + slot) * blocks
            target[first + second] = terms[row : row + blocks].astype(BF16)
        row = (3 * second + 1) * blocks
        middle[second] = terms[row : row + blocks]


def spread_down(row, count):
    return jnp.broadcast_to(row.astype(F32), (count, row.shape[1])).T


def start_kernel(chunks, sizes, weights, v, fill, home, far, count,
                 held, up, down, middle, middle_diag, live, pick_home, put_home, pick_far, put_far,
                 vectors, products, sums, arrived):
    size_first, size_second = sizes
    blocks, tile = v.shape
    npairs = weights.shape[0]
    per_chunk = npairs // chunks

    def copy(index):
        part = pl.ds(index * per_chunk, per_chunk)
        return pltpu.make_async_copy(weights.at[part], held.at[part], arrived.at[index])

    for index in range(chunks):
        copy(index).start()
    lane = lax.broadcasted_iota(jnp.int32, (blocks, tile), 1)
    mask = jnp.where(lane.astype(F32) < spread_down(fill[...], tile), 1.0, 0.0)
    live[...] = mask
    q = (mask * v[...]).astype(BF16)
    up[0] = q
    down[0] = q

    first_index, second_index = lax.axis_index("gx"), lax.axis_index("gy")
    kept = lax.broadcasted_iota(jnp.int32, (1, npairs), 1) < count[0]
    far_block = far[...]
    far_device = lax.div(far_block, blocks)
    slot_first = lax.rem(lax.div(far_device, size_second) - first_index + 1 + size_first, size_first)
    slot_second = lax.rem(lax.rem(far_device, size_second) - second_index + 1 + size_second, size_second)
    far_row = jnp.where(kept, (slot_second * 3 + slot_first) * blocks + lax.rem(far_block, blocks), -1)
    home_row = jnp.where(kept, home[...] - (first_index * size_second + second_index) * blocks, -1)
    across = lax.broadcasted_iota(jnp.int32, (npairs, blocks), 1).astype(F32)
    along = lax.broadcasted_iota(jnp.int32, (blocks, npairs), 0)

    def mark(same):
        return jnp.where(same, 1.0, 0.0).astype(BF16)

    pick_home[...] = mark(across == spread_down(home_row, blocks))
    vectors[...] = dot_rows(pick_home[...], q).astype(BF16)
    put_home[...] = mark(along == home_row)
    far_column = spread_down(far_row, blocks)
    for slot in range(9):
        part = slice(slot * blocks, slot * blocks + blocks)
        pick_far[:, part] = mark(across + float(slot * blocks) == far_column)
        put_far[part, :] = mark(along + slot * blocks == far_row)

    pair_products(held, vectors, products, sums, False, chunks, lambda index: copy(index).wait())
    send_terms(placed(put_far[...], products[...]), up, down, middle, 1)
    send_terms(placed(put_far[...], sums[...]), up, down, middle_diag, 4)


def toward_home(weights, near, pick_far, put_home, vectors, products, sums):
    vectors[...] = dot_rows(pick_far[...], near[...]).astype(BF16)
    pair_products(weights, vectors, products, sums, True, 3)
    return placed(put_home[...], products[...])


def away_next(weights, v, live, pick_home, put_far, up, down, middle, vectors, products):
    q = (live * v).astype(BF16)
    up[0] = q
    down[0] = q
    vectors[...] = dot_rows(pick_home[...], q).astype(BF16)
    pair_products(weights, vectors, products, None, False, 3)
    send_terms(placed(put_far[...], products[...]), up, down, middle, 1)


def second_kernel(weights, near, pick_far, put_home, pick_home, put_far, far_total, far_diag, v, live, compress,
                  after, diag_out, up, down, middle, vectors, products, sums):
    total = toward_home(weights, near, pick_far, put_home, vectors, products, sums) + far_total[...]
    mask = live[...]
    diag = compress[...] + mask * (placed(put_home[...], sums[...]) + far_diag[...])
    diag_out[...] = diag
    result = (diag - SHIFT) * v[...] - mask * total
    after[...] = result
    away_next(weights, result, mask, pick_home, put_far, up, down, middle, vectors, products)


def third_kernel(weights, near, pick_far, put_home, pick_home, put_far, far_total, v, live, diag,
                 after, up, down, middle, vectors, products):
    total = toward_home(weights, near, pick_far, put_home, vectors, products, None) + far_total[...]
    mask = live[...]
    result = (diag[...] - SHIFT) * v[...] - mask * total
    after[...] = result
    away_next(weights, result, mask, pick_home, put_far, up, down, middle, vectors, products)


def last_kernel(weights, near, pick_far, put_home, far_total, v0, v1, v2, live, diag, image, dots, vectors, products):
    sums, mask = far_total[...], live[...]
    total = toward_home(weights, near, pick_far, put_home, vectors, products, None) + sums
    a, b, c = v0[...], v1[...], v2[...]
    scaled = diag[...] * c
    image[...] = scaled - mask * total
    energy = c * (scaled - 2.0 * mask * sums)
    lane = lax.broadcasted_iota(jnp.int32, (1, 128), 1)
    row = jnp.zeros((1, 128), F32)
    for index, product in enumerate((a * a, a * b, a * c, b * b, b * c, c * c, energy)):
        result = jnp.sum(jnp.sum(product, axis=0, keepdims=True), axis=1, keepdims=True)
        row = jnp.where(lane == index, result, row)
    dots[...] = jnp.broadcast_to(row, dots.shape)


def finish_kernel(dots, v0, v1, v2, a2, solution_field, residual):
    row = jnp.sum(dots[...], axis=0, keepdims=True)
    lane = lax.broadcasted_iota(jnp.int32, row.shape, 1)

    def entry(index):
        return jnp.sum(jnp.where(lane == index, row, 0.0), axis=1, keepdims=True)

    g00, g01, g02, g11, g12, g22, m22 = (entry(index) for index in range(7))
    gram = ((g00, g01, g02), (g01, g11, g12), (g02, g12, g22))
    m00 = g01 + SHIFT * g00
    m01 = g11 + SHIFT * g01
    m11 = g12 + SHIFT * g11
    m02 = g12 + SHIFT * g02
    m12 = g22 + SHIFT * g12
    energies = ((m00, m01, m02), (m01, m11, m12), (m02, m12, m22))

    def form(matrix, p):
        return sum(p[i] * p[j] * matrix[i][j] for i in range(len(p)) for j in range(len(p)))

    def step_size(norm, p):
        floor = jnp.maximum(COMPRESS_MIN * norm, 1e-30)
        return norm / jnp.maximum(form(energies, p), floor)

    def moved(r, alpha, p):
        image = [SHIFT * p[i] + (p[i - 1] if i else 0.0) for i in range(len(p))] + [p[-1]]
        return [(r[i] if i < len(r) else 0.0) - alpha * image[i] for i in range(len(image))]

    def turned(r, beta, p):
        return [r[i] + beta * p[i] if i < len(p) else r[i] for i in range(len(r))]

    def norm_of(r):
        return jnp.maximum(form(gram, r), 0.0)

    one = jnp.ones_like(g00)
    p0 = [one]
    alpha0 = step_size(g00, p0)
    r1 = moved([one], alpha0, p0)
    n1 = norm_of(r1)
    p1 = turned(r1, n1 / jnp.maximum(g00, 1e-30), p0)
    alpha1 = step_size(n1, p1)
    r2 = moved(r1, alpha1, p1)
    n2 = norm_of(r2)
    p2 = turned(r2, n2 / jnp.maximum(n1, 1e-30), p1)
    alpha2 = step_size(n2, p2)
    x = [alpha0 * p0[0] + alpha1 * p1[0] + alpha2 * p2[0], alpha1 * p1[1] + alpha2 * p2[1], alpha2 * p2[2]]
    images = [SHIFT * p2[0], p2[0] + SHIFT * p2[1], p2[1]]
    r = [r2[i] - alpha2 * images[i] for i in range(3)]
    a, b, c = v0[...], v1[...], v2[...]
    solution_field[...] = x[0] * a + x[1] * b + x[2] * c
    residual[...] = r[0] * a + r[1] * b + r[2] * c - (alpha2 * p2[2]) * a2[...]


def shifted(value, axis, step):
    count = lax.axis_size(axis)
    return lax.ppermute(value, axis, [(source, (source + step) % count) for source in range(count)])


def call(kernel, outs, scratch, args, in_hbm=(), in_smem=()):
    spaces = [pl.ANY if i in in_hbm else pltpu.SMEM if i in in_smem else pltpu.VMEM for i in range(len(args))]
    vmem = pl.BlockSpec(memory_space=pltpu.VMEM)
    return pl.pallas_call(
        kernel,
        out_shape=outs,
        in_specs=[pl.BlockSpec(memory_space=space) for space in spaces],
        out_specs=[vmem] * len(outs),
        scratch_shapes=scratch,
        compiler_params=pltpu.CompilerParams(vmem_limit_bytes=36 * 2**20),
    )(*args)


def exchanged(up, down, middle, middle_diag=None):
    low, high = shifted(up, "gx", 1), shifted(down, "gx", -1)
    column = jnp.stack([low[0], up[0], high[0]])

    def summed(second, first, own):
        return own[second] + low[first + second].astype(F32) + high[first + second].astype(F32)

    kinds = [(1, middle)] if middle_diag is None else [(1, middle), (4, middle_diag)]

    def message(second):
        sums = [summed(second, first, own).astype(BF16)[None] for first, own in kinds]
        return jnp.concatenate([column, *sums])

    from_low, from_high = shifted(message(2), "gy", 1), shifted(message(0), "gy", -1)
    near = jnp.concatenate([from_low[:3], column, from_high[:3]])
    near = near.reshape(-1, near.shape[-1])
    totals = [
        summed(1, first, own) + from_low[3 + kind].astype(F32) + from_high[3 + kind].astype(F32)
        for kind, (first, own) in enumerate(kinds)
    ]
    return near, *totals


def on_device(right_side, compress, block_fill, pair_home, pair_far, pair_count, weights):
    blocks, tile = right_side.shape
    npairs = weights.shape[0]
    size_first, size_second = lax.axis_size("gx"), lax.axis_size("gy")

    def shape(*dims, dtype=F32):
        return jax.ShapeDtypeStruct(dims, dtype)

    own_shape = shape(blocks, tile)
    middle_shape = shape(3, blocks, tile)
    rows16, rows32 = pltpu.VMEM((npairs, tile), BF16), pltpu.VMEM((npairs, tile), F32)

    def slabs(count):
        return shape(count, blocks, tile, dtype=BF16)

    chunks = 6
    pick = shape(npairs, blocks, dtype=BF16), shape(blocks, npairs, dtype=BF16)
    pick += shape(npairs, 9 * blocks, dtype=BF16), shape(9 * blocks, npairs, dtype=BF16)
    held, up, down, middle, middle_diag, live, pick_home, put_home, pick_far, put_far = call(
        functools.partial(start_kernel, chunks, (size_first, size_second)),
        [pltpu.VMEM(weights.shape, BF16), slabs(7), slabs(7), middle_shape, middle_shape, own_shape, *pick],
        [rows16, rows32, rows32, pltpu.SemaphoreType.DMA((chunks,))],
        (weights, right_side, block_fill[None], pair_home[None], pair_far[None], pair_count),
        in_hbm=(0,),
        in_smem=(5,),
    )
    held = pltpu.with_memory_space_constraint(held, pltpu.VMEM)
    near, far_total, far_diag = exchanged(up, down, middle, middle_diag)
    v0 = right_side
    v1, diag, up, down, middle = call(
        second_kernel,
        [own_shape, own_shape, slabs(4), slabs(4), middle_shape],
        [rows16, rows32, rows32],
        (held, near, pick_far, put_home, pick_home, put_far, far_total, far_diag, v0, live, compress),
    )
    near, far_total = exchanged(up, down, middle)
    v2, up, down, middle = call(
        third_kernel,
        [own_shape, slabs(4), slabs(4), middle_shape],
        [rows16, rows32],
        (held, near, pick_far, put_home, pick_home, put_far, far_total, v1, live, diag),
    )
    near, far_total = exchanged(up, down, middle)
    image, dots = call(
        last_kernel,
        [own_shape, shape(size_first * size_second, tile)],
        [rows16, rows32],
        (held, near, pick_far, put_home, far_total, v0, v1, v2, live, diag),
    )
    dots = lax.all_to_all(dots, BOTH, 0, 0, tiled=True)
    return tuple(call(finish_kernel, [own_shape, own_shape], [], (dots, v0, v1, v2, image)))


def solution(mesh):
    return jax.shard_map(
        on_device,
        mesh=mesh,
        in_specs=(
            P(BOTH, None),
            P(BOTH, None),
            P(BOTH),
            P(BOTH),
            P(BOTH),
            P(BOTH),
            P(BOTH, None, None),
        ),
        out_specs=(P(BOTH, None), P(BOTH, None)),
        check_vma=False,
    )
```

```python
import functools

import jax
import jax.numpy as jnp
from jax import lax
from jax.experimental import pallas as pl
from jax.experimental.pallas import tpu as pltpu
from jax.sharding import PartitionSpec as P

SHIFT = 4.0
COMPRESS_MIN = 0.5
GROUP = 16
F32 = jnp.float32
BF16 = jnp.bfloat16
BOTH = ("gx", "gy")


def dot_rows(a, b):
    return lax.dot_general(a, b, (((1,), (0,)), ((), ())), preferred_element_type=F32)


def placed(onehot, terms):
    high = terms.astype(BF16)
    low = (terms - high.astype(F32)).astype(BF16)
    both = dot_rows(onehot, jnp.concatenate([high, low], axis=1))
    return both[:, :128] + both[:, 128:]


def pair_products(weights, vectors, out, sums, chunks, arrive=None):
    per_chunk = weights.shape[0] // GROUP // chunks
    sublane = lax.broadcasted_iota(jnp.int32, (8, 128), 0)
    zero = jnp.zeros((8, 128), F32)

    def group(base):
        rows = pl.ds(base, GROUP)
        left = vectors[rows, :]
        if sums is not None:
            left = jnp.concatenate([left, jnp.ones((GROUP, 128), BF16)])
        results = [[zero, zero], [zero, zero]]
        for pair in range(0, GROUP, 2):
            first, second = weights[base + pair], weights[base + pair + 1]
            product = dot_rows(left, jnp.concatenate([first, second], axis=1))
            for which in range(2):
                half, here = (pair + which) // 8, sublane == (pair + which) % 8
                columns = slice(128 * which, 128 * which + 128)
                for kind in range(1 if sums is None else 2):
                    start = GROUP * kind + 8 * half
                    results[kind][half] = jnp.where(here, product[start : start + 8, columns], results[kind][half])
        out[rows, :] = jnp.concatenate(results[0])
        if sums is not None:
            sums[rows, :] = jnp.concatenate(results[1])

    def chunk(index, carry):
        if arrive is not None:
            arrive(index)
        for inner in range(per_chunk):
            group(pl.multiple_of((index * per_chunk + inner) * GROUP, GROUP))
        return carry

    lax.fori_loop(0, chunks, chunk, 0)


def send_terms(terms, up, down, middle, first):
    blocks = up.shape[1]
    for second in range(3):
        for target, slot in ((down, 0), (up, 2)):
            row = (3 * second + slot) * blocks
            target[first + second] = terms[row : row + blocks].astype(BF16)
        row = (3 * second + 1) * blocks
        middle[second] = terms[row : row + blocks]


def spread_down(row, count):
    return jnp.broadcast_to(row.astype(F32), (count, row.shape[1])).T


def start_kernel(chunks, weights, v_hbm, fill_hbm, home_hbm, far_hbm, count,
                 held, up, down, middle, middle_diag, live, pick_home, put_home, pick_far, put_far,
                 v, fill, home, far, vectors, products, sums, arrived, ready):
    blocks, tile = v.shape
    npairs = weights.shape[0]
    per_chunk = npairs // chunks
    small = [
        pltpu.make_async_copy(source, target, ready.at[index])
        for index, (source, target) in enumerate(
            ((fill_hbm, fill), (v_hbm, v), (home_hbm, home), (far_hbm, far))
        )
    ]

    def copy(index):
        part = pl.ds(index * per_chunk, per_chunk)
        return pltpu.make_async_copy(weights.at[part], held.at[part], arrived.at[index])

    for each in small:
        each.start()
    for index in range(chunks):
        copy(index).start()
    for each in small:
        each.wait()
    lane = lax.broadcasted_iota(jnp.int32, (blocks, tile), 1)
    mask = jnp.where(lane.astype(F32) < spread_down(fill[...].reshape(1, blocks), tile), 1.0, 0.0)
    live[...] = mask
    q = (mask * v[...]).astype(BF16)
    up[0] = q
    down[0] = q

    first_index, second_index = lax.axis_index("gx"), lax.axis_index("gy")
    size_second = lax.axis_size("gy")
    kept = lax.broadcasted_iota(jnp.int32, (1, npairs), 1) < count[0]
    far_block = far[...].reshape(1, npairs)
    far_device = lax.div(far_block, blocks)

    def slot_of(there, here):
        partner = here + 1 - 2 * lax.rem(here, 2)
        return jnp.where(there == here, 1, jnp.where(there == partner, 0, 2))

    slot_first = slot_of(lax.div(far_device, size_second), first_index)
    slot_second = slot_of(lax.rem(far_device, size_second), second_index)
    far_row = jnp.where(kept, (slot_second * 3 + slot_first) * blocks + lax.rem(far_block, blocks), -1)
    home_row = home[...].reshape(1, npairs) - (first_index * size_second + second_index) * blocks
    home_row = jnp.where(kept, home_row, -1)
    across = lax.broadcasted_iota(jnp.int32, (npairs, blocks), 1).astype(F32)
    along = lax.broadcasted_iota(jnp.int32, (blocks, npairs), 0)

    def mark(same):
        return jnp.where(same, 1.0, 0.0).astype(BF16)

    pick_home[...] = mark(across == spread_down(home_row, blocks))
    vectors[...] = dot_rows(pick_home[...], q).astype(BF16)
    put_home[...] = mark(along == home_row)
    far_column = spread_down(far_row, blocks)
    for slot in range(9):
        part = slice(slot * blocks, slot * blocks + blocks)
        pick_far[:, part] = mark(across + float(slot * blocks) == far_column)
        put_far[part, :] = mark(along + slot * blocks == far_row)

    pair_products(held, vectors, products, sums, chunks, lambda index: copy(index).wait())
    send_terms(placed(put_far[...], products[...]), up, down, middle, 1)
    send_terms(placed(put_far[...], sums[...]), up, down, middle_diag, 4)


def flip_kernel(weights, flipped, token):
    step = 16
    token[...] = jnp.zeros_like(token)

    def some(index, carry):
        for inner in range(step):
            flipped[index * step + inner] = weights[index * step + inner].T
        return carry

    lax.fori_loop(0, weights.shape[0] // step, some, 0)


def toward_home(flipped, near, pick_far, put_home, vectors, products, sums):
    vectors[...] = dot_rows(pick_far[...], near[...]).astype(BF16)
    pair_products(flipped, vectors, products, sums, 3)
    return placed(put_home[...], products[...])


def away_next(weights, v, live, pick_home, put_far, up, down, middle, vectors, products):
    q = (live * v).astype(BF16)
    up[0] = q
    down[0] = q
    vectors[...] = dot_rows(pick_home[...], q).astype(BF16)
    pair_products(weights, vectors, products, None, 3)
    send_terms(placed(put_far[...], products[...]), up, down, middle, 1)


def second_kernel(weights, flipped, near, pick_far, put_home, pick_home, put_far, far_total, far_diag, v, live, compress,
                  after, diag_out, up, down, middle, vectors, products, sums):
    total = toward_home(flipped, near, pick_far, put_home, vectors, products, sums) + far_total[...]
    mask = live[...]
    diag = compress[...] + mask * (placed(put_home[...], sums[...]) + far_diag[...])
    diag_out[...] = diag
    result = (diag - SHIFT) * v[...] - mask * total
    after[...] = result
    away_next(weights, result, mask, pick_home, put_far, up, down, middle, vectors, products)


def third_kernel(weights, flipped, near, pick_far, put_home, pick_home, put_far, far_total, v, live, diag,
                 after, up, down, middle, vectors, products):
    total = toward_home(flipped, near, pick_far, put_home, vectors, products, None) + far_total[...]
    mask = live[...]
    result = (diag[...] - SHIFT) * v[...] - mask * total
    after[...] = result
    away_next(weights, result, mask, pick_home, put_far, up, down, middle, vectors, products)


def last_kernel(flipped, near, pick_far, put_home, far_total, v0, v1, v2, live, diag, image, dots, vectors, products):
    sums, mask = far_total[...], live[...]
    total = toward_home(flipped, near, pick_far, put_home, vectors, products, None) + sums
    a, b, c = v0[...], v1[...], v2[...]
    scaled = diag[...] * c
    image[...] = scaled - mask * total
    energy = c * (scaled - 2.0 * mask * sums)
    lane = lax.broadcasted_iota(jnp.int32, (1, 128), 1)
    row = jnp.zeros((1, 128), F32)
    for index, product in enumerate((a * a, a * b, a * c, b * b, b * c, c * c, energy)):
        result = jnp.sum(jnp.sum(product, axis=0, keepdims=True), axis=1, keepdims=True)
        row = jnp.where(lane == index, result, row)
    dots[...] = jnp.broadcast_to(row, dots.shape)


def finish_kernel(dots, v0, v1, v2, a2, solution_field, residual):
    row = jnp.sum(dots[...], axis=0, keepdims=True)
    lane = lax.broadcasted_iota(jnp.int32, row.shape, 1)

    def entry(index):
        return jnp.sum(jnp.where(lane == index, row, 0.0), axis=1, keepdims=True)

    g00, g01, g02, g11, g12, g22, m22 = (entry(index) for index in range(7))
    gram = ((g00, g01, g02), (g01, g11, g12), (g02, g12, g22))
    m00 = g01 + SHIFT * g00
    m01 = g11 + SHIFT * g01
    m11 = g12 + SHIFT * g11
    m02 = g12 + SHIFT * g02
    m12 = g22 + SHIFT * g12
    energies = ((m00, m01, m02), (m01, m11, m12), (m02, m12, m22))

    def form(matrix, p):
        return sum(p[i] * p[j] * matrix[i][j] for i in range(len(p)) for j in range(len(p)))

    def step_size(norm, p):
        floor = jnp.maximum(COMPRESS_MIN * norm, 1e-30)
        return norm / jnp.maximum(form(energies, p), floor)

    def moved(r, alpha, p):
        image = [SHIFT * p[i] + (p[i - 1] if i else 0.0) for i in range(len(p))] + [p[-1]]
        return [(r[i] if i < len(r) else 0.0) - alpha * image[i] for i in range(len(image))]

    def turned(r, beta, p):
        return [r[i] + beta * p[i] if i < len(p) else r[i] for i in range(len(r))]

    def norm_of(r):
        return jnp.maximum(form(gram, r), 0.0)

    one = jnp.ones_like(g00)
    p0 = [one]
    alpha0 = step_size(g00, p0)
    r1 = moved([one], alpha0, p0)
    n1 = norm_of(r1)
    p1 = turned(r1, n1 / jnp.maximum(g00, 1e-30), p0)
    alpha1 = step_size(n1, p1)
    r2 = moved(r1, alpha1, p1)
    n2 = norm_of(r2)
    p2 = turned(r2, n2 / jnp.maximum(n1, 1e-30), p1)
    alpha2 = step_size(n2, p2)
    x = [alpha0 * p0[0] + alpha1 * p1[0] + alpha2 * p2[0], alpha1 * p1[1] + alpha2 * p2[1], alpha2 * p2[2]]
    images = [SHIFT * p2[0], p2[0] + SHIFT * p2[1], p2[1]]
    r = [r2[i] - alpha2 * images[i] for i in range(3)]
    a, b, c = v0[...], v1[...], v2[...]
    solution_field[...] = x[0] * a + x[1] * b + x[2] * c
    residual[...] = r[0] * a + r[1] * b + r[2] * c - (alpha2 * p2[2]) * a2[...]


def swapped(value, axis, offset):
    count = lax.axis_size(axis)
    pairs = [(place, (((place + offset) ^ 1) - offset) % count) for place in range(count)]
    return lax.ppermute(value, axis, pairs)


def call(kernel, outs, scratch, args, in_hbm=(), in_smem=(), cost=None):
    args = [pltpu.with_memory_space_constraint(x, pltpu.HBM) if i in in_hbm else x for i, x in enumerate(args)]
    spaces = [pltpu.HBM if i in in_hbm else pltpu.SMEM if i in in_smem else pltpu.VMEM for i in range(len(args))]
    vmem = pl.BlockSpec(memory_space=pltpu.VMEM)
    return pl.pallas_call(
        kernel,
        out_shape=outs,
        in_specs=[pl.BlockSpec(memory_space=space) for space in spaces],
        out_specs=[vmem] * len(outs),
        scratch_shapes=scratch,
        cost_estimate=cost,
        compiler_params=pltpu.CompilerParams(vmem_limit_bytes=12 * 2**20),
    )(*args)


def exchanged(up, down, middle, middle_diag=None, token=None):
    low, high = swapped(down, "gx", 0), swapped(up, "gx", 1)
    column = jnp.stack([low[0], up[0], high[0]])

    def summed(second, first, own):
        return own[second] + low[first + second].astype(F32) + high[first + second].astype(F32)

    kinds = [(1, middle)] if middle_diag is None else [(1, middle), (4, middle_diag)]

    def message(second):
        sums = [summed(second, first, own) for first, own in kinds]
        if token is not None:
            sums = [each + token[:1] for each in sums]
        sums = [each.astype(BF16)[None] for each in sums]
        return jnp.concatenate([column, *sums])

    from_low, from_high = swapped(message(0), "gy", 0), swapped(message(2), "gy", 1)
    near = jnp.concatenate([from_low[:3], column, from_high[:3]])
    near = near.reshape(-1, near.shape[-1])
    totals = [
        summed(1, first, own) + from_low[3 + kind].astype(F32) + from_high[3 + kind].astype(F32)
        for kind, (first, own) in enumerate(kinds)
    ]
    return near, *totals


def on_device(right_side, compress, block_fill, pair_home, pair_far, pair_count, weights):
    blocks, tile = right_side.shape
    npairs = weights.shape[0]
    size_first, size_second = lax.axis_size("gx"), lax.axis_size("gy")

    def shape(*dims, dtype=F32):
        return jax.ShapeDtypeStruct(dims, dtype)

    own_shape = shape(blocks, tile)
    middle_shape = shape(3, blocks, tile)
    rows16, rows32 = pltpu.VMEM((npairs, tile), BF16), pltpu.VMEM((npairs, tile), F32)

    def slabs(count):
        return shape(count, blocks, tile, dtype=BF16)

    chunks = 6
    pick = shape(npairs, blocks, dtype=BF16), shape(blocks, npairs, dtype=BF16)
    pick += shape(npairs, 9 * blocks, dtype=BF16), shape(9 * blocks, npairs, dtype=BF16)
    held, up, down, middle, middle_diag, live, pick_home, put_home, pick_far, put_far = call(
        functools.partial(start_kernel, chunks),
        [pltpu.VMEM(weights.shape, BF16), slabs(7), slabs(7), middle_shape, middle_shape, own_shape, *pick],
        [
            pltpu.VMEM((blocks, tile), F32), pltpu.VMEM((blocks,), jnp.int32), pltpu.VMEM((npairs,), jnp.int32),
            pltpu.VMEM((npairs,), jnp.int32), rows16, rows32, rows32,
            pltpu.SemaphoreType.DMA((chunks,)), pltpu.SemaphoreType.DMA((4,)),
        ],
        (weights, right_side, block_fill, pair_home, pair_far, pair_count),
        in_hbm=range(5),
        in_smem=(5,),
    )
    held = pltpu.with_memory_space_constraint(held, pltpu.VMEM)
    flipped, token = call(
        flip_kernel,
        [pltpu.VMEM(weights.shape, BF16), shape(8, tile)],
        [],
        (held,),
        cost=pl.CostEstimate(flops=0, bytes_accessed=weights.size * 6, transcendentals=0),
    )
    flipped = pltpu.with_memory_space_constraint(flipped, pltpu.VMEM)
    near, far_total, far_diag = exchanged(up, down, middle, middle_diag, token)
    v0 = right_side
    v1, diag, up, down, middle = call(
        second_kernel,
        [own_shape, own_shape, slabs(4), slabs(4), middle_shape],
        [rows16, rows32, rows32],
        (held, flipped, near, pick_far, put_home, pick_home, put_far, far_total, far_diag, v0, live, compress),
    )
    near, far_total = exchanged(up, down, middle)
    v2, up, down, middle = call(
        third_kernel,
        [own_shape, slabs(4), slabs(4), middle_shape],
        [rows16, rows32],
        (held, flipped, near, pick_far, put_home, pick_home, put_far, far_total, v1, live, diag),
    )
    near, far_total = exchanged(up, down, middle)
    image, dots = call(
        last_kernel,
        [own_shape, shape(size_first * size_second, tile)],
        [rows16, rows32],
        (flipped, near, pick_far, put_home, far_total, v0, v1, v2, live, diag),
    )
    dots = lax.all_to_all(dots, BOTH, 0, 0, tiled=True)
    return tuple(call(finish_kernel, [own_shape, own_shape], [], (dots, v0, v1, v2, image)))


def solution(mesh):
    return jax.shard_map(
        on_device,
        mesh=mesh,
        in_specs=(
            P(BOTH, None),
            P(BOTH, None),
            P(BOTH),
            P(BOTH),
            P(BOTH),
            P(BOTH),
            P(BOTH, None, None),
        ),
        out_specs=(P(BOTH, None), P(BOTH, None)),
        check_vma=False,
    )
```

```python
import functools

import jax
import jax.numpy as jnp
from jax import lax
from jax.experimental import pallas as pl
from jax.experimental.pallas import tpu as pltpu
from jax.sharding import PartitionSpec as P

SHIFT = 4.0
COMPRESS_MIN = 0.5
GROUP = 16
START_CHUNKS = 3
F32 = jnp.float32
BF16 = jnp.bfloat16
BOTH = ("gx", "gy")


def dot_rows(a, b):
    return lax.dot_general(a, b, (((1,), (0,)), ((), ())), preferred_element_type=F32)


def placed(onehot, terms):
    high = terms.astype(BF16)
    low = (terms - high.astype(F32)).astype(BF16)
    both = dot_rows(onehot, jnp.concatenate([high, low], axis=1))
    return both[:, :128] + both[:, 128:]


def pair_products(weights, vectors, out, sums, chunks, arrive=None):
    per_chunk = weights.shape[0] // GROUP // chunks
    sublane = lax.broadcasted_iota(jnp.int32, (8, 128), 0)
    zero = jnp.zeros((8, 128), F32)

    def group(base):
        rows = pl.ds(base, GROUP)
        left = vectors[rows, :]
        if sums is not None:
            left = jnp.concatenate([left, jnp.ones((GROUP, 128), BF16)])
        results = [[zero, zero], [zero, zero]]
        for pair in range(0, GROUP, 2):
            first, second = weights[base + pair], weights[base + pair + 1]
            product = dot_rows(left, jnp.concatenate([first, second], axis=1))
            for which in range(2):
                half, here = (pair + which) // 8, sublane == (pair + which) % 8
                columns = slice(128 * which, 128 * which + 128)
                for kind in range(1 if sums is None else 2):
                    start = GROUP * kind + 8 * half
                    results[kind][half] = jnp.where(here, product[start : start + 8, columns], results[kind][half])
        out[rows, :] = jnp.concatenate(results[0])
        if sums is not None:
            sums[rows, :] = jnp.concatenate(results[1])

    for index in range(chunks):
        if arrive is not None:
            arrive(index)
        for inner in range(per_chunk):
            group((index * per_chunk + inner) * GROUP)


def send_terms(terms, up, down, middle, first):
    blocks = up.shape[1]
    for second in range(3):
        for target, slot in ((down, 0), (up, 2)):
            row = (3 * second + slot) * blocks
            target[first + second] = terms[row : row + blocks].astype(BF16)
        row = (3 * second + 1) * blocks
        middle[second] = terms[row : row + blocks]


def spread_down(row, count):
    return jnp.broadcast_to(row.astype(F32), (count, row.shape[1])).T


def start_kernel(chunks, weights, v_hbm, fill_hbm, home_hbm, far_hbm, count,
                 held, up, down, middle, middle_diag, live, pick_home, put_home, pick_far, put_far,
                 v, fill, home, far, vectors, products, sums, arrived, ready):
    blocks, tile = v.shape
    npairs = weights.shape[0]
    per_chunk = npairs // chunks
    small = [
        pltpu.make_async_copy(source, target, ready.at[index])
        for index, (source, target) in enumerate(
            ((fill_hbm, fill), (v_hbm, v), (home_hbm, home), (far_hbm, far))
        )
    ]

    def copy(index):
        part = pl.ds(index * per_chunk, per_chunk)
        return pltpu.make_async_copy(weights.at[part], held.at[part], arrived.at[index])

    for each in small:
        each.start()
    for index in range(chunks):
        copy(index).start()
    for each in small:
        each.wait()
    lane = lax.broadcasted_iota(jnp.int32, (blocks, tile), 1)
    mask = jnp.where(lane.astype(F32) < spread_down(fill[...].reshape(1, blocks), tile), 1.0, 0.0)
    live[...] = mask
    q = (mask * v[...]).astype(BF16)
    up[0] = q
    down[0] = q

    first_index, second_index = lax.axis_index("gx"), lax.axis_index("gy")
    size_second = lax.axis_size("gy")
    kept = lax.broadcasted_iota(jnp.int32, (1, npairs), 1) < count[0]
    far_block = far[...].reshape(1, npairs)
    far_device = lax.div(far_block, blocks)

    def slot_of(there, here):
        partner = here + 1 - 2 * lax.rem(here, 2)
        return jnp.where(there == here, 1, jnp.where(there == partner, 0, 2))

    slot_first = slot_of(lax.div(far_device, size_second), first_index)
    slot_second = slot_of(lax.rem(far_device, size_second), second_index)
    far_row = jnp.where(kept, (slot_second * 3 + slot_first) * blocks + lax.rem(far_block, blocks), -1)
    home_row = home[...].reshape(1, npairs) - (first_index * size_second + second_index) * blocks
    home_row = jnp.where(kept, home_row, -1)
    across = lax.broadcasted_iota(jnp.int32, (npairs, blocks), 1).astype(F32)
    along = lax.broadcasted_iota(jnp.int32, (blocks, npairs), 0)

    def mark(same):
        return jnp.where(same, 1.0, 0.0).astype(BF16)

    pick_home[...] = mark(across == spread_down(home_row, blocks))
    vectors[...] = dot_rows(pick_home[...], q).astype(BF16)
    put_home[...] = mark(along == home_row)
    far_column = spread_down(far_row, blocks)
    for slot in range(9):
        part = slice(slot * blocks, slot * blocks + blocks)
        pick_far[:, part] = mark(across + float(slot * blocks) == far_column)
        put_far[part, :] = mark(along + slot * blocks == far_row)

    pair_products(held, vectors, products, sums, chunks, lambda index: copy(index).wait())
    both = jnp.concatenate([products[...].astype(BF16), sums[...].astype(BF16)], axis=1)
    both = dot_rows(put_far[...], both)
    send_terms(both[:, :tile], up, down, middle, 1)
    send_terms(both[:, tile:], up, down, middle_diag, 4)


def flip_kernel(weights, flipped, token):
    step = 16
    token[...] = jnp.zeros_like(token)

    def some(index, carry):
        for inner in range(step):
            flipped[index * step + inner] = weights[index * step + inner].T
        return carry

    lax.fori_loop(0, weights.shape[0] // step, some, 0)


def toward_home(flipped, near, pick_far, put_home, vectors, products, sums):
    vectors[...] = dot_rows(pick_far[...], near[...]).astype(BF16)
    pair_products(flipped, vectors, products, sums, 1)
    return placed(put_home[...], products[...])


def away_next(weights, v, live, pick_home, put_far, up, down, middle, vectors, products):
    q = (live * v).astype(BF16)
    up[0] = q
    down[0] = q
    vectors[...] = dot_rows(pick_home[...], q).astype(BF16)
    pair_products(weights, vectors, products, None, 1)
    send_terms(dot_rows(put_far[...], products[...].astype(BF16)), up, down, middle, 1)


def second_kernel(weights, flipped, near, pick_far, put_home, pick_home, put_far, far_total, far_diag, v, live, compress,
                  after, diag_out, up, down, middle, vectors, products, sums):
    total = toward_home(flipped, near, pick_far, put_home, vectors, products, sums) + far_total[...]
    mask = live[...]
    diag = compress[...] + mask * (placed(put_home[...], sums[...]) + far_diag[...])
    diag_out[...] = diag
    result = (diag - SHIFT) * v[...] - mask * total
    after[...] = result
    away_next(weights, result, mask, pick_home, put_far, up, down, middle, vectors, products)


def third_kernel(weights, flipped, near, pick_far, put_home, pick_home, put_far, far_total, v, live, diag,
                 after, up, down, middle, vectors, products):
    total = toward_home(flipped, near, pick_far, put_home, vectors, products, None) + far_total[...]
    mask = live[...]
    result = (diag[...] - SHIFT) * v[...] - mask * total
    after[...] = result
    away_next(weights, result, mask, pick_home, put_far, up, down, middle, vectors, products)


def last_kernel(flipped, near, pick_far, put_home, far_total, v0, v1, v2, live, diag, image, dots, vectors, products):
    sums, mask = far_total[...], live[...]
    total = toward_home(flipped, near, pick_far, put_home, vectors, products, None) + sums
    a, b, c = v0[...], v1[...], v2[...]
    scaled = diag[...] * c
    image[...] = scaled - mask * total
    energy = c * (scaled - 2.0 * mask * sums)
    lane = lax.broadcasted_iota(jnp.int32, (1, 128), 1)
    row = jnp.zeros((1, 128), F32)
    for index, product in enumerate((a * a, a * b, a * c, b * b, b * c, c * c, energy)):
        result = jnp.sum(jnp.sum(product, axis=0, keepdims=True), axis=1, keepdims=True)
        row = jnp.where(lane == index, result, row)
    dots[...] = jnp.broadcast_to(row, dots.shape)


def finish_kernel(dots, v0, v1, v2, a2, solution_field, residual):
    row = jnp.sum(dots[...], axis=0, keepdims=True)
    lane = lax.broadcasted_iota(jnp.int32, row.shape, 1)

    def entry(index):
        return jnp.sum(jnp.where(lane == index, row, 0.0), axis=1, keepdims=True)

    g00, g01, g02, g11, g12, g22, m22 = (entry(index) for index in range(7))
    gram = ((g00, g01, g02), (g01, g11, g12), (g02, g12, g22))
    m00 = g01 + SHIFT * g00
    m01 = g11 + SHIFT * g01
    m11 = g12 + SHIFT * g11
    m02 = g12 + SHIFT * g02
    m12 = g22 + SHIFT * g12
    energies = ((m00, m01, m02), (m01, m11, m12), (m02, m12, m22))

    def form(matrix, p):
        return sum(p[i] * p[j] * matrix[i][j] for i in range(len(p)) for j in range(len(p)))

    def step_size(norm, p):
        floor = jnp.maximum(COMPRESS_MIN * norm, 1e-30)
        return norm / jnp.maximum(form(energies, p), floor)

    def moved(r, alpha, p):
        image = [SHIFT * p[i] + (p[i - 1] if i else 0.0) for i in range(len(p))] + [p[-1]]
        return [(r[i] if i < len(r) else 0.0) - alpha * image[i] for i in range(len(image))]

    def turned(r, beta, p):
        return [r[i] + beta * p[i] if i < len(p) else r[i] for i in range(len(r))]

    def norm_of(r):
        return jnp.maximum(form(gram, r), 0.0)

    one = jnp.ones_like(g00)
    p0 = [one]
    alpha0 = step_size(g00, p0)
    r1 = moved([one], alpha0, p0)
    n1 = norm_of(r1)
    p1 = turned(r1, n1 / jnp.maximum(g00, 1e-30), p0)
    alpha1 = step_size(n1, p1)
    r2 = moved(r1, alpha1, p1)
    n2 = norm_of(r2)
    p2 = turned(r2, n2 / jnp.maximum(n1, 1e-30), p1)
    alpha2 = step_size(n2, p2)
    x = [alpha0 * p0[0] + alpha1 * p1[0] + alpha2 * p2[0], alpha1 * p1[1] + alpha2 * p2[1], alpha2 * p2[2]]
    images = [SHIFT * p2[0], p2[0] + SHIFT * p2[1], p2[1]]
    r = [r2[i] - alpha2 * images[i] for i in range(3)]
    a, b, c = v0[...], v1[...], v2[...]
    solution_field[...] = x[0] * a + x[1] * b + x[2] * c
    residual[...] = r[0] * a + r[1] * b + r[2] * c - (alpha2 * p2[2]) * a2[...]


def swapped(value, axis, offset):
    count = lax.axis_size(axis)
    pairs = [(place, (((place + offset) ^ 1) - offset) % count) for place in range(count)]
    return lax.ppermute(value, axis, pairs)


def call(kernel, outs, scratch, args, in_hbm=(), in_smem=(), cost=None):
    args = [pltpu.with_memory_space_constraint(x, pltpu.HBM) if i in in_hbm else x for i, x in enumerate(args)]
    spaces = [pltpu.HBM if i in in_hbm else pltpu.SMEM if i in in_smem else pltpu.VMEM for i in range(len(args))]
    vmem = pl.BlockSpec(memory_space=pltpu.VMEM)
    return pl.pallas_call(
        kernel,
        out_shape=outs,
        in_specs=[pl.BlockSpec(memory_space=space) for space in spaces],
        out_specs=[vmem] * len(outs),
        scratch_shapes=scratch,
        cost_estimate=cost,
        compiler_params=pltpu.CompilerParams(vmem_limit_bytes=12 * 2**20),
    )(*args)


def exchanged(up, down, middle, middle_diag=None, token=None):
    low, high = swapped(down, "gx", 0), swapped(up, "gx", 1)
    column = jnp.stack([low[0], up[0], high[0]])

    def summed(second, first, own):
        return own[second] + low[first + second].astype(F32) + high[first + second].astype(F32)

    kinds = [(1, middle)] if middle_diag is None else [(1, middle), (4, middle_diag)]

    def message(second):
        sums = [summed(second, first, own) for first, own in kinds]
        if token is not None:
            sums = [each + token[:1] for each in sums]
        sums = [each.astype(BF16)[None] for each in sums]
        return jnp.concatenate([column, *sums])

    from_low, from_high = swapped(message(0), "gy", 0), swapped(message(2), "gy", 1)
    near = jnp.concatenate([from_low[:3], column, from_high[:3]])
    near = near.reshape(-1, near.shape[-1])
    totals = [
        summed(1, first, own) + from_low[3 + kind].astype(F32) + from_high[3 + kind].astype(F32)
        for kind, (first, own) in enumerate(kinds)
    ]
    return near, *totals


def on_device(right_side, compress, block_fill, pair_home, pair_far, pair_count, weights):
    blocks, tile = right_side.shape
    npairs = weights.shape[0]
    size_first, size_second = lax.axis_size("gx"), lax.axis_size("gy")

    def shape(*dims, dtype=F32):
        return jax.ShapeDtypeStruct(dims, dtype)

    own_shape = shape(blocks, tile)
    middle_shape = shape(3, blocks, tile)
    rows16, rows32 = pltpu.VMEM((npairs, tile), BF16), pltpu.VMEM((npairs, tile), F32)

    def slabs(count):
        return shape(count, blocks, tile, dtype=BF16)

    chunks = START_CHUNKS
    pick = shape(npairs, blocks, dtype=BF16), shape(blocks, npairs, dtype=BF16)
    pick += shape(npairs, 9 * blocks, dtype=BF16), shape(9 * blocks, npairs, dtype=BF16)
    held, up, down, middle, middle_diag, live, pick_home, put_home, pick_far, put_far = call(
        functools.partial(start_kernel, chunks),
        [pltpu.VMEM(weights.shape, BF16), slabs(7), slabs(7), middle_shape, middle_shape, own_shape, *pick],
        [
            pltpu.VMEM((blocks, tile), F32), pltpu.VMEM((blocks,), jnp.int32), pltpu.VMEM((npairs,), jnp.int32),
            pltpu.VMEM((npairs,), jnp.int32), rows16, rows32, rows32,
            pltpu.SemaphoreType.DMA((chunks,)), pltpu.SemaphoreType.DMA((4,)),
        ],
        (weights, right_side, block_fill, pair_home, pair_far, pair_count),
        in_hbm=range(5),
        in_smem=(5,),
    )
    held = pltpu.with_memory_space_constraint(held, pltpu.VMEM)
    flipped, token = call(
        flip_kernel,
        [pltpu.VMEM(weights.shape, BF16), shape(8, tile)],
        [],
        (held,),
        cost=pl.CostEstimate(flops=0, bytes_accessed=weights.size * 6, transcendentals=0),
    )
    flipped = pltpu.with_memory_space_constraint(flipped, pltpu.VMEM)
    near, far_total, far_diag = exchanged(up, down, middle, middle_diag, token)
    v0 = right_side
    v1, diag, up, down, middle = call(
        second_kernel,
        [own_shape, own_shape, slabs(4), slabs(4), middle_shape],
        [rows16, rows32, rows32],
        (held, flipped, near, pick_far, put_home, pick_home, put_far, far_total, far_diag, v0, live, compress),
    )
    near, far_total = exchanged(up, down, middle)
    v2, up, down, middle = call(
        third_kernel,
        [own_shape, slabs(4), slabs(4), middle_shape],
        [rows16, rows32],
        (held, flipped, near, pick_far, put_home, pick_home, put_far, far_total, v1, live, diag),
    )
    near, far_total = exchanged(up, down, middle)
    image, dots = call(
        last_kernel,
        [own_shape, shape(size_first * size_second, tile)],
        [rows16, rows32],
        (flipped, near, pick_far, put_home, far_total, v0, v1, v2, live, diag),
    )
    dots = lax.all_to_all(dots, BOTH, 0, 0, tiled=True)
    return tuple(call(finish_kernel, [own_shape, own_shape], [], (dots, v0, v1, v2, image)))


def solution(mesh):
    return jax.shard_map(
        on_device,
        mesh=mesh,
        in_specs=(
            P(BOTH, None),
            P(BOTH, None),
            P(BOTH),
            P(BOTH),
            P(BOTH),
            P(BOTH),
            P(BOTH, None, None),
        ),
        out_specs=(P(BOTH, None), P(BOTH, None)),
        check_vma=False,
    )
```

```python
import jax
import jax.numpy as jnp
from jax import lax
from jax.experimental import pallas as pl
from jax.experimental.pallas import tpu as pltpu
from jax.sharding import PartitionSpec as P

SHIFT = 4.0
COMPRESS_MIN = 0.5
GROUP = 16
CHUNK_STARTS = (0, 256)
F32 = jnp.float32
BF16 = jnp.bfloat16
BOTH = ("gx", "gy")


def dot_rows(a, b):
    return lax.dot_general(a, b, (((1,), (0,)), ((), ())), preferred_element_type=F32)


def placed(onehot, terms):
    high = terms.astype(BF16)
    low = (terms - high.astype(F32)).astype(BF16)
    both = dot_rows(onehot, jnp.concatenate([high, low], axis=1))
    return both[:, :128] + both[:, 128:]


def pair_products(weights, vectors, out, sums, aside=0, arrive=None):
    sublane = lax.broadcasted_iota(jnp.int32, (8, 128), 0)
    zero = jnp.zeros((8, 128), F32)
    columns = vectors[...].astype(F32).T if aside else None

    def group(base):
        rows = pl.ds(base, GROUP)
        left = vectors[rows, :]
        if sums is not None:
            left = jnp.concatenate([left, jnp.ones((GROUP, 128), BF16)])
        results = [[zero, zero], [zero, zero]]

        def put(kind, pair, value):
            half = pair // 8
            results[kind][half] = jnp.where(sublane == pair % 8, value, results[kind][half])

        for pair in range(0, GROUP - aside, 2):
            product = dot_rows(left, jnp.concatenate([weights[base + pair], weights[base + pair + 1]], axis=1))
            for which in range(2):
                lanes = slice(128 * which, 128 * which + 128)
                for kind in range(1 if sums is None else 2):
                    start = GROUP * kind + (pair + which) // 8 * 8
                    put(kind, pair + which, product[start : start + 8, lanes])
        for pair in range(GROUP - aside, GROUP):
            tile = weights[base + pair].astype(F32)
            put(0, pair, jnp.sum(tile * columns[:, base + pair : base + pair + 1], axis=0, keepdims=True))
            if sums is not None:
                put(1, pair, jnp.sum(tile, axis=0, keepdims=True))
        out[rows, :] = jnp.concatenate(results[0])
        if sums is not None:
            sums[rows, :] = jnp.concatenate(results[1])

    for base in range(0, weights.shape[0], GROUP):
        if arrive is not None:
            arrive(base)
        group(base)


def send_terms(terms, up, down, middle, first):
    blocks = up.shape[1]
    for second in range(3):
        for target, slot in ((down, 0), (up, 2)):
            row = (3 * second + slot) * blocks
            target[first + second] = terms[row : row + blocks].astype(BF16)
        row = (3 * second + 1) * blocks
        middle[second] = terms[row : row + blocks]


def spread_down(row, count):
    return jnp.broadcast_to(row.astype(F32), (count, row.shape[1])).T


def start_kernel(weights, v_hbm, fill_hbm, home_hbm, far_hbm, count,
                 held, up, down, middle, middle_diag, live, pick_home, put_home, pick_far, put_far,
                 v, fill, home, far, vectors, products, sums, arrived, ready):
    blocks, tile = v.shape
    npairs = weights.shape[0]
    small = [
        pltpu.make_async_copy(source, target, ready.at[index])
        for index, (source, target) in enumerate(
            ((fill_hbm, fill), (v_hbm, v), (home_hbm, home), (far_hbm, far))
        )
    ]

    def copy(index):
        first, last = (*CHUNK_STARTS, npairs)[index : index + 2]
        part = pl.ds(first, last - first)
        return pltpu.make_async_copy(weights.at[part], held.at[part], arrived.at[index])

    for each in small:
        each.start()
    for index in range(len(CHUNK_STARTS)):
        copy(index).start()
    for each in small:
        each.wait()
    lane = lax.broadcasted_iota(jnp.int32, (blocks, tile), 1)
    mask = jnp.where(lane.astype(F32) < spread_down(fill[...].reshape(1, blocks), tile), 1.0, 0.0)
    live[...] = mask
    q = (mask * v[...]).astype(BF16)
    up[0] = q
    down[0] = q

    first_index, second_index = lax.axis_index("gx"), lax.axis_index("gy")
    size_second = lax.axis_size("gy")
    kept = lax.broadcasted_iota(jnp.int32, (1, npairs), 1) < count[0]
    far_block = far[...].reshape(1, npairs)
    far_device = lax.div(far_block, blocks)

    def slot_of(there, here):
        partner = here + 1 - 2 * lax.rem(here, 2)
        return jnp.where(there == here, 1, jnp.where(there == partner, 0, 2))

    slot_first = slot_of(lax.div(far_device, size_second), first_index)
    slot_second = slot_of(lax.rem(far_device, size_second), second_index)
    far_row = jnp.where(kept, (slot_second * 3 + slot_first) * blocks + lax.rem(far_block, blocks), -1)
    home_row = home[...].reshape(1, npairs) - (first_index * size_second + second_index) * blocks
    home_row = jnp.where(kept, home_row, -1)
    across = lax.broadcasted_iota(jnp.int32, (npairs, blocks), 1).astype(F32)
    along = lax.broadcasted_iota(jnp.int32, (blocks, npairs), 0)

    def mark(same):
        return jnp.where(same, 1.0, 0.0).astype(BF16)

    pick_home[...] = mark(across == spread_down(home_row, blocks))
    vectors[...] = dot_rows(pick_home[...], q).astype(BF16)
    put_home[...] = mark(along == home_row)
    far_column = spread_down(far_row, blocks)
    for slot in range(9):
        part = slice(slot * blocks, slot * blocks + blocks)
        pick_far[:, part] = mark(across + float(slot * blocks) == far_column)
        put_far[part, :] = mark(along + slot * blocks == far_row)


    def arrive(base):
        if base in CHUNK_STARTS:
            copy(CHUNK_STARTS.index(base)).wait()

    pair_products(held, vectors, products, sums, 0, arrive)
    both = jnp.concatenate([products[...].astype(BF16), sums[...].astype(BF16)], axis=1)
    both = dot_rows(put_far[...], both)
    send_terms(both[:, :tile], up, down, middle, 1)
    send_terms(both[:, tile:], up, down, middle_diag, 4)


def flip_kernel(weights, flipped, token):
    step = 16
    token[...] = jnp.zeros_like(token)

    def some(index, carry):
        for inner in range(step):
            flipped[index * step + inner] = weights[index * step + inner].T
        return carry

    lax.fori_loop(0, weights.shape[0] // step, some, 0)


def toward_home(flipped, near, pick_far, put_home, vectors, products, sums):
    vectors[...] = dot_rows(pick_far[...], near[...]).astype(BF16)
    pair_products(flipped, vectors, products, sums, 4 if sums is None else 2)
    return placed(put_home[...], products[...])


def away_next(weights, v, live, pick_home, put_far, up, down, middle, vectors, products):
    q = (live * v).astype(BF16)
    up[0] = q
    down[0] = q
    vectors[...] = dot_rows(pick_home[...], q).astype(BF16)
    pair_products(weights, vectors, products, None, 4)
    send_terms(dot_rows(put_far[...], products[...].astype(BF16)), up, down, middle, 1)


def second_kernel(weights, flipped, near, pick_far, put_home, pick_home, put_far, far_total, far_diag, v, live, compress,
                  after, diag_out, up, down, middle, vectors, products, sums):
    total = toward_home(flipped, near, pick_far, put_home, vectors, products, sums) + far_total[...]
    mask = live[...]
    diag = compress[...] + mask * (placed(put_home[...], sums[...]) + far_diag[...])
    diag_out[...] = diag
    result = (diag - SHIFT) * v[...] - mask * total
    after[...] = result
    away_next(weights, result, mask, pick_home, put_far, up, down, middle, vectors, products)


def third_kernel(weights, flipped, near, pick_far, put_home, pick_home, put_far, far_total, v, live, diag,
                 after, up, down, middle, vectors, products):
    total = toward_home(flipped, near, pick_far, put_home, vectors, products, None) + far_total[...]
    mask = live[...]
    result = (diag[...] - SHIFT) * v[...] - mask * total
    after[...] = result
    away_next(weights, result, mask, pick_home, put_far, up, down, middle, vectors, products)


def last_kernel(flipped, near, pick_far, put_home, far_total, v0, v1, v2, live, diag, image, dots, vectors, products):
    sums, mask = far_total[...], live[...]
    total = toward_home(flipped, near, pick_far, put_home, vectors, products, None) + sums
    a, b, c = v0[...], v1[...], v2[...]
    scaled = diag[...] * c
    image[...] = scaled - mask * total
    energy = c * (scaled - 2.0 * mask * sums)
    lane = lax.broadcasted_iota(jnp.int32, (1, 128), 1)
    row = jnp.zeros((1, 128), F32)
    for index, product in enumerate((a * a, a * b, a * c, b * b, b * c, c * c, energy)):
        result = jnp.sum(jnp.sum(product, axis=0, keepdims=True), axis=1, keepdims=True)
        row = jnp.where(lane == index, result, row)
    dots[...] = jnp.broadcast_to(row, dots.shape)


def finish_kernel(dots, v0, v1, v2, a2, solution_field, residual):
    row = jnp.sum(dots[...], axis=0, keepdims=True)
    lane = lax.broadcasted_iota(jnp.int32, row.shape, 1)

    def entry(index):
        return jnp.sum(jnp.where(lane == index, row, 0.0), axis=1, keepdims=True)

    g00, g01, g02, g11, g12, g22, m22 = (entry(index) for index in range(7))
    gram = ((g00, g01, g02), (g01, g11, g12), (g02, g12, g22))
    m00 = g01 + SHIFT * g00
    m01 = g11 + SHIFT * g01
    m11 = g12 + SHIFT * g11
    m02 = g12 + SHIFT * g02
    m12 = g22 + SHIFT * g12
    energies = ((m00, m01, m02), (m01, m11, m12), (m02, m12, m22))

    def form(matrix, p):
        return sum(p[i] * p[j] * matrix[i][j] for i in range(len(p)) for j in range(len(p)))

    def step_size(norm, p):
        floor = jnp.maximum(COMPRESS_MIN * norm, 1e-30)
        return norm / jnp.maximum(form(energies, p), floor)

    def moved(r, alpha, p):
        image = [SHIFT * p[i] + (p[i - 1] if i else 0.0) for i in range(len(p))] + [p[-1]]
        return [(r[i] if i < len(r) else 0.0) - alpha * image[i] for i in range(len(image))]

    def turned(r, beta, p):
        return [r[i] + beta * p[i] if i < len(p) else r[i] for i in range(len(r))]

    def norm_of(r):
        return jnp.maximum(form(gram, r), 0.0)

    one = jnp.ones_like(g00)
    p0 = [one]
    alpha0 = step_size(g00, p0)
    r1 = moved([one], alpha0, p0)
    n1 = norm_of(r1)
    p1 = turned(r1, n1 / jnp.maximum(g00, 1e-30), p0)
    alpha1 = step_size(n1, p1)
    r2 = moved(r1, alpha1, p1)
    n2 = norm_of(r2)
    p2 = turned(r2, n2 / jnp.maximum(n1, 1e-30), p1)
    alpha2 = step_size(n2, p2)
    x = [alpha0 * p0[0] + alpha1 * p1[0] + alpha2 * p2[0], alpha1 * p1[1] + alpha2 * p2[1], alpha2 * p2[2]]
    images = [SHIFT * p2[0], p2[0] + SHIFT * p2[1], p2[1]]
    r = [r2[i] - alpha2 * images[i] for i in range(3)]
    a, b, c = v0[...], v1[...], v2[...]
    solution_field[...] = x[0] * a + x[1] * b + x[2] * c
    residual[...] = r[0] * a + r[1] * b + r[2] * c - (alpha2 * p2[2]) * a2[...]


def swapped(value, axis, offset):
    count = lax.axis_size(axis)
    pairs = [(place, (((place + offset) ^ 1) - offset) % count) for place in range(count)]
    return lax.ppermute(value, axis, pairs)


def call(kernel, outs, scratch, args, in_hbm=(), in_smem=(), cost=None):
    args = [pltpu.with_memory_space_constraint(x, pltpu.HBM) if i in in_hbm else x for i, x in enumerate(args)]
    spaces = [pltpu.HBM if i in in_hbm else pltpu.SMEM if i in in_smem else pltpu.VMEM for i in range(len(args))]
    vmem = pl.BlockSpec(memory_space=pltpu.VMEM)
    return pl.pallas_call(
        kernel,
        out_shape=outs,
        in_specs=[pl.BlockSpec(memory_space=space) for space in spaces],
        out_specs=[vmem] * len(outs),
        scratch_shapes=scratch,
        cost_estimate=cost,
        compiler_params=pltpu.CompilerParams(vmem_limit_bytes=12 * 2**20),
    )(*args)


def exchanged(up, down, middle, middle_diag=None, token=None):
    low, high = swapped(down, "gx", 0), swapped(up, "gx", 1)
    column = jnp.stack([low[0], up[0], high[0]])

    def summed(second, first, own):
        return own[second] + low[first + second].astype(F32) + high[first + second].astype(F32)

    kinds = [(1, middle)] if middle_diag is None else [(1, middle), (4, middle_diag)]

    def message(second):
        sums = [summed(second, first, own) for first, own in kinds]
        if token is not None:
            sums = [each + token[:1] for each in sums]
        sums = [each.astype(BF16)[None] for each in sums]
        return jnp.concatenate([column, *sums])

    from_low, from_high = swapped(message(0), "gy", 0), swapped(message(2), "gy", 1)
    near = jnp.concatenate([from_low[:3], column, from_high[:3]])
    near = near.reshape(-1, near.shape[-1])
    totals = [
        summed(1, first, own) + from_low[3 + kind].astype(F32) + from_high[3 + kind].astype(F32)
        for kind, (first, own) in enumerate(kinds)
    ]
    return near, *totals


def on_device(right_side, compress, block_fill, pair_home, pair_far, pair_count, weights):
    blocks, tile = right_side.shape
    npairs = weights.shape[0]
    size_first, size_second = lax.axis_size("gx"), lax.axis_size("gy")

    def shape(*dims, dtype=F32):
        return jax.ShapeDtypeStruct(dims, dtype)

    own_shape = shape(blocks, tile)
    middle_shape = shape(3, blocks, tile)
    rows16, rows32 = pltpu.VMEM((npairs, tile), BF16), pltpu.VMEM((npairs, tile), F32)

    def slabs(count):
        return shape(count, blocks, tile, dtype=BF16)

    pick = shape(npairs, blocks, dtype=BF16), shape(blocks, npairs, dtype=BF16)
    pick += shape(npairs, 9 * blocks, dtype=BF16), shape(9 * blocks, npairs, dtype=BF16)
    held, up, down, middle, middle_diag, live, pick_home, put_home, pick_far, put_far = call(
        start_kernel,
        [pltpu.VMEM(weights.shape, BF16), slabs(7), slabs(7), middle_shape, middle_shape, own_shape, *pick],
        [
            pltpu.VMEM((blocks, tile), F32), pltpu.VMEM((blocks,), jnp.int32), pltpu.VMEM((npairs,), jnp.int32),
            pltpu.VMEM((npairs,), jnp.int32), rows16, rows32, rows32,
            pltpu.SemaphoreType.DMA((len(CHUNK_STARTS),)), pltpu.SemaphoreType.DMA((4,)),
        ],
        (weights, right_side, block_fill, pair_home, pair_far, pair_count),
        in_hbm=range(5),
        in_smem=(5,),
    )
    held = pltpu.with_memory_space_constraint(held, pltpu.VMEM)
    flipped, token = call(
        flip_kernel,
        [pltpu.VMEM(weights.shape, BF16), shape(8, tile)],
        [],
        (held,),
        cost=pl.CostEstimate(flops=0, bytes_accessed=weights.size * 6, transcendentals=0),
    )
    flipped = pltpu.with_memory_space_constraint(flipped, pltpu.VMEM)
    near, far_total, far_diag = exchanged(up, down, middle, middle_diag, token)
    v0 = right_side
    v1, diag, up, down, middle = call(
        second_kernel,
        [own_shape, own_shape, slabs(4), slabs(4), middle_shape],
        [rows16, rows32, rows32],
        (held, flipped, near, pick_far, put_home, pick_home, put_far, far_total, far_diag, v0, live, compress),
    )
    near, far_total = exchanged(up, down, middle)
    v2, up, down, middle = call(
        third_kernel,
        [own_shape, slabs(4), slabs(4), middle_shape],
        [rows16, rows32],
        (held, flipped, near, pick_far, put_home, pick_home, put_far, far_total, v1, live, diag),
    )
    near, far_total = exchanged(up, down, middle)
    image, dots = call(
        last_kernel,
        [own_shape, shape(size_first * size_second, tile)],
        [rows16, rows32],
        (flipped, near, pick_far, put_home, far_total, v0, v1, v2, live, diag),
    )
    dots = lax.all_to_all(dots, BOTH, 0, 0, tiled=True)
    return tuple(call(finish_kernel, [own_shape, own_shape], [], (dots, v0, v1, v2, image)))


def solution(mesh):
    return jax.shard_map(
        on_device,
        mesh=mesh,
        in_specs=(
            P(BOTH, None),
            P(BOTH, None),
            P(BOTH),
            P(BOTH),
            P(BOTH),
            P(BOTH),
            P(BOTH, None, None),
        ),
        out_specs=(P(BOTH, None), P(BOTH, None)),
        check_vma=False,
    )
```

```python
import jax
import jax.numpy as jnp
from jax import lax
from jax.experimental import pallas as pl
from jax.experimental.pallas import tpu as pltpu
from jax.sharding import PartitionSpec as P

SHIFT = 4.0
COMPRESS_MIN = 0.5
GROUP = 16
CHUNK_STARTS = (0, 256)
F32 = jnp.float32
BF16 = jnp.bfloat16
BOTH = ("gx", "gy")


def dot_rows(a, b):
    return lax.dot_general(a, b, (((1,), (0,)), ((), ())), preferred_element_type=F32)


def placed(onehot, terms):
    high = terms.astype(BF16)
    low = (terms - high.astype(F32)).astype(BF16)
    both = dot_rows(onehot, jnp.concatenate([high, low], axis=1))
    return both[:, :128] + both[:, 128:]


def pair_products(weights, vectors, out, sums, aside=0, arrive=None):
    sublane = lax.broadcasted_iota(jnp.int32, (8, 128), 0)
    zero = jnp.zeros((8, 128), F32)
    columns = vectors[...].astype(F32).T if aside else None

    def group(base):
        rows = pl.ds(base, GROUP)
        left = vectors[rows, :]
        if sums is not None:
            left = jnp.concatenate([left, jnp.ones((GROUP, 128), BF16)])
        results = [[zero, zero], [zero, zero]]

        def put(kind, pair, value):
            half = pair // 8
            results[kind][half] = jnp.where(sublane == pair % 8, value, results[kind][half])

        for pair in range(0, GROUP - aside, 2):
            product = dot_rows(left, jnp.concatenate([weights[base + pair], weights[base + pair + 1]], axis=1))
            for which in range(2):
                lanes = slice(128 * which, 128 * which + 128)
                for kind in range(1 if sums is None else 2):
                    start = GROUP * kind + (pair + which) // 8 * 8
                    put(kind, pair + which, product[start : start + 8, lanes])
        for pair in range(GROUP - aside, GROUP):
            tile = weights[base + pair].astype(F32)
            put(0, pair, jnp.sum(tile * columns[:, base + pair : base + pair + 1], axis=0, keepdims=True))
            if sums is not None:
                put(1, pair, jnp.sum(tile, axis=0, keepdims=True))
        out[rows, :] = jnp.concatenate(results[0])
        if sums is not None:
            sums[rows, :] = jnp.concatenate(results[1])

    for base in range(0, weights.shape[0], GROUP):
        if arrive is not None:
            arrive(base)
        group(base)


def send_terms(terms, up, down, middle, first):
    blocks = up.shape[1]
    for second in range(3):
        for target, slot in ((down, 0), (up, 2)):
            row = (3 * second + slot) * blocks
            target[first + second] = terms[row : row + blocks].astype(BF16)
        row = (3 * second + 1) * blocks
        middle[second] = terms[row : row + blocks]


def spread_down(row, count):
    return jnp.broadcast_to(row.astype(F32), (count, row.shape[1])).T


def lane_numbers(rows):
    return lax.broadcasted_iota(jnp.int32, (rows, 128), 1).astype(F32)


def mark(same):
    return jnp.where(same, 1.0, 0.0).astype(BF16)


def start_kernel(weights, v_hbm, fill_hbm, home_hbm, far_hbm, count,
                 held, up, down, middle, middle_diag, live, pick_home, put_far, routes,
                 v, fill, home, far, vectors, products, sums, arrived, ready):
    blocks, tile = v.shape
    npairs = weights.shape[0]
    small = [
        pltpu.make_async_copy(source, target, ready.at[index])
        for index, (source, target) in enumerate(
            ((fill_hbm, fill), (v_hbm, v), (home_hbm, home), (far_hbm, far))
        )
    ]

    def copy(index):
        first, last = (*CHUNK_STARTS, npairs)[index : index + 2]
        part = pl.ds(first, last - first)
        return pltpu.make_async_copy(weights.at[part], held.at[part], arrived.at[index])

    for each in small:
        each.start()
    for index in range(len(CHUNK_STARTS)):
        copy(index).start()
    for each in small:
        each.wait()
    lane = lax.broadcasted_iota(jnp.int32, (blocks, tile), 1)
    mask = jnp.where(lane.astype(F32) < spread_down(fill[...].reshape(1, blocks), tile), 1.0, 0.0)
    live[...] = mask
    q = (mask * v[...]).astype(BF16)
    up[0] = q
    down[0] = q

    first_index, second_index = lax.axis_index("gx"), lax.axis_index("gy")
    size_second = lax.axis_size("gy")
    kept = lax.broadcasted_iota(jnp.int32, (1, npairs), 1) < count[0]
    far_block = far[...].reshape(1, npairs)
    far_device = lax.div(far_block, blocks)

    def slot_of(there, here):
        partner = here + 1 - 2 * lax.rem(here, 2)
        return jnp.where(there == here, 1, jnp.where(there == partner, 0, 2))

    slot_first = slot_of(lax.div(far_device, size_second), first_index)
    slot_second = slot_of(lax.rem(far_device, size_second), second_index)
    far_row = jnp.where(kept, (slot_second * 3 + slot_first) * blocks + lax.rem(far_block, blocks), -1)
    home_row = home[...].reshape(1, npairs) - (first_index * size_second + second_index) * blocks
    home_row = jnp.where(kept, home_row, -1)
    routes[0:1, :] = far_row
    routes[1:2, :] = home_row
    pick_home[...] = mark(lane_numbers(npairs) == spread_down(home_row, blocks))
    vectors[...] = dot_rows(pick_home[...], q).astype(BF16)
    along = lax.broadcasted_iota(jnp.int32, (blocks, npairs), 0)
    for part in range(9):
        rows = slice(part * blocks, part * blocks + blocks)
        put_far[rows, :] = mark(along + part * blocks == far_row)

    def arrive(base):
        if base in CHUNK_STARTS:
            copy(CHUNK_STARTS.index(base)).wait()

    pair_products(held, vectors, products, sums, 0, arrive)
    both = jnp.concatenate([products[...].astype(BF16), sums[...].astype(BF16)], axis=1)
    both = dot_rows(put_far[...], both)
    send_terms(both[:, :tile], up, down, middle, 1)
    send_terms(both[:, tile:], up, down, middle_diag, 4)


def flip_kernel(weights, routes, flipped, token, put_home, pick_far):
    step = 16
    token[...] = jnp.zeros_like(token)
    blocks, npairs = put_home.shape
    put_home[...] = mark(lax.broadcasted_iota(jnp.int32, (blocks, npairs), 0) == routes[1:2, :])
    far_column = spread_down(routes[0:1, :], blocks)
    for part in range(9):
        columns = slice(part * blocks, part * blocks + blocks)
        pick_far[:, columns] = mark(lane_numbers(npairs) + float(part * blocks) == far_column)

    def some(index, carry):
        for inner in range(step):
            flipped[index * step + inner] = weights[index * step + inner].T
        return carry

    lax.fori_loop(0, weights.shape[0] // step, some, 0)


def toward_home(flipped, near, pick_far, put_home, vectors, products, sums):
    vectors[...] = dot_rows(pick_far[...], near[...]).astype(BF16)
    pair_products(flipped, vectors, products, sums, 4 if sums is None else 2)
    return placed(put_home[...], products[...])


def away_next(weights, v, live, pick_home, put_far, up, down, middle, vectors, products):
    q = (live * v).astype(BF16)
    up[0] = q
    down[0] = q
    vectors[...] = dot_rows(pick_home[...], q).astype(BF16)
    pair_products(weights, vectors, products, None, 4)
    send_terms(dot_rows(put_far[...], products[...].astype(BF16)), up, down, middle, 1)


def second_kernel(weights, flipped, near, pick_far, put_home, pick_home, put_far, far_total, far_diag, v, live, compress,
                  after, diag_out, up, down, middle, vectors, products, sums):
    total = toward_home(flipped, near, pick_far, put_home, vectors, products, sums) + far_total[...]
    mask = live[...]
    diag = compress[...] + mask * (placed(put_home[...], sums[...]) + far_diag[...])
    diag_out[...] = diag
    result = (diag - SHIFT) * v[...] - mask * total
    after[...] = result
    away_next(weights, result, mask, pick_home, put_far, up, down, middle, vectors, products)


def third_kernel(weights, flipped, near, pick_far, put_home, pick_home, put_far, far_total, v, live, diag,
                 after, up, down, middle, vectors, products):
    total = toward_home(flipped, near, pick_far, put_home, vectors, products, None) + far_total[...]
    mask = live[...]
    result = (diag[...] - SHIFT) * v[...] - mask * total
    after[...] = result
    away_next(weights, result, mask, pick_home, put_far, up, down, middle, vectors, products)


def last_kernel(flipped, near, pick_far, put_home, far_total, v0, v1, v2, live, diag, image, dots, vectors, products):
    sums, mask = far_total[...], live[...]
    total = toward_home(flipped, near, pick_far, put_home, vectors, products, None) + sums
    a, b, c = v0[...], v1[...], v2[...]
    scaled = diag[...] * c
    image[...] = scaled - mask * total
    energy = c * (scaled - 2.0 * mask * sums)
    lane = lax.broadcasted_iota(jnp.int32, (1, 128), 1)
    row = jnp.zeros((1, 128), F32)
    for index, product in enumerate((a * a, a * b, a * c, b * b, b * c, c * c, energy)):
        result = jnp.sum(jnp.sum(product, axis=0, keepdims=True), axis=1, keepdims=True)
        row = jnp.where(lane == index, result, row)
    dots[...] = jnp.broadcast_to(row, dots.shape)


def finish_kernel(dots, v0, v1, v2, a2, solution_field, residual):
    row = jnp.sum(dots[...], axis=0, keepdims=True)
    lane = lax.broadcasted_iota(jnp.int32, row.shape, 1)

    def entry(index):
        return jnp.sum(jnp.where(lane == index, row, 0.0), axis=1, keepdims=True)

    g00, g01, g02, g11, g12, g22, m22 = (entry(index) for index in range(7))
    gram = ((g00, g01, g02), (g01, g11, g12), (g02, g12, g22))
    m00 = g01 + SHIFT * g00
    m01 = g11 + SHIFT * g01
    m11 = g12 + SHIFT * g11
    m02 = g12 + SHIFT * g02
    m12 = g22 + SHIFT * g12
    energies = ((m00, m01, m02), (m01, m11, m12), (m02, m12, m22))

    def form(matrix, p):
        return sum(p[i] * p[j] * matrix[i][j] for i in range(len(p)) for j in range(len(p)))

    def step_size(norm, p):
        floor = jnp.maximum(COMPRESS_MIN * norm, 1e-30)
        return norm / jnp.maximum(form(energies, p), floor)

    def moved(r, alpha, p):
        image = [SHIFT * p[i] + (p[i - 1] if i else 0.0) for i in range(len(p))] + [p[-1]]
        return [(r[i] if i < len(r) else 0.0) - alpha * image[i] for i in range(len(image))]

    def turned(r, beta, p):
        return [r[i] + beta * p[i] if i < len(p) else r[i] for i in range(len(r))]

    def norm_of(r):
        return jnp.maximum(form(gram, r), 0.0)

    one = jnp.ones_like(g00)
    p0 = [one]
    alpha0 = step_size(g00, p0)
    r1 = moved([one], alpha0, p0)
    n1 = norm_of(r1)
    p1 = turned(r1, n1 / jnp.maximum(g00, 1e-30), p0)
    alpha1 = step_size(n1, p1)
    r2 = moved(r1, alpha1, p1)
    n2 = norm_of(r2)
    p2 = turned(r2, n2 / jnp.maximum(n1, 1e-30), p1)
    alpha2 = step_size(n2, p2)
    x = [alpha0 * p0[0] + alpha1 * p1[0] + alpha2 * p2[0], alpha1 * p1[1] + alpha2 * p2[1], alpha2 * p2[2]]
    images = [SHIFT * p2[0], p2[0] + SHIFT * p2[1], p2[1]]
    r = [r2[i] - alpha2 * images[i] for i in range(3)]
    a, b, c = v0[...], v1[...], v2[...]
    solution_field[...] = x[0] * a + x[1] * b + x[2] * c
    residual[...] = r[0] * a + r[1] * b + r[2] * c - (alpha2 * p2[2]) * a2[...]


def swapped(value, axis, offset):
    count = lax.axis_size(axis)
    pairs = [(place, (((place + offset) ^ 1) - offset) % count) for place in range(count)]
    return lax.ppermute(value, axis, pairs)


def call(kernel, outs, scratch, args, in_hbm=(), in_smem=(), cost=None):
    args = [pltpu.with_memory_space_constraint(x, pltpu.HBM) if i in in_hbm else x for i, x in enumerate(args)]
    spaces = [pltpu.HBM if i in in_hbm else pltpu.SMEM if i in in_smem else pltpu.VMEM for i in range(len(args))]
    vmem = pl.BlockSpec(memory_space=pltpu.VMEM)
    return pl.pallas_call(
        kernel,
        out_shape=outs,
        in_specs=[pl.BlockSpec(memory_space=space) for space in spaces],
        out_specs=[vmem] * len(outs),
        scratch_shapes=scratch,
        cost_estimate=cost,
        compiler_params=pltpu.CompilerParams(vmem_limit_bytes=12 * 2**20),
    )(*args)


def exchanged(up, down, middle, middle_diag=None, token=None):
    low, high = swapped(down, "gx", 0), swapped(up, "gx", 1)
    column = jnp.stack([low[0], up[0], high[0]])

    def summed(second, first, own):
        return own[second] + low[first + second].astype(F32) + high[first + second].astype(F32)

    kinds = [(1, middle)] if middle_diag is None else [(1, middle), (4, middle_diag)]

    def message(second):
        sums = [summed(second, first, own) for first, own in kinds]
        if token is not None:
            sums = [each + token[:1] for each in sums]
        sums = [each.astype(BF16)[None] for each in sums]
        return jnp.concatenate([column, *sums])

    from_low, from_high = swapped(message(0), "gy", 0), swapped(message(2), "gy", 1)
    near = jnp.concatenate([from_low[:3], column, from_high[:3]])
    near = near.reshape(-1, near.shape[-1])
    totals = [
        summed(1, first, own) + from_low[3 + kind].astype(F32) + from_high[3 + kind].astype(F32)
        for kind, (first, own) in enumerate(kinds)
    ]
    return near, *totals


def on_device(right_side, compress, block_fill, pair_home, pair_far, pair_count, weights):
    blocks, tile = right_side.shape
    npairs = weights.shape[0]
    size_first, size_second = lax.axis_size("gx"), lax.axis_size("gy")

    def shape(*dims, dtype=F32):
        return jax.ShapeDtypeStruct(dims, dtype)

    own_shape = shape(blocks, tile)
    middle_shape = shape(3, blocks, tile)
    rows16, rows32 = pltpu.VMEM((npairs, tile), BF16), pltpu.VMEM((npairs, tile), F32)

    def slabs(count):
        return shape(count, blocks, tile, dtype=BF16)

    held, up, down, middle, middle_diag, live, pick_home, put_far, routes = call(
        start_kernel,
        [pltpu.VMEM(weights.shape, BF16), slabs(7), slabs(7), middle_shape, middle_shape, own_shape,
         shape(npairs, blocks, dtype=BF16), shape(9 * blocks, npairs, dtype=BF16), shape(2, npairs, dtype=jnp.int32)],
        [
            pltpu.VMEM((blocks, tile), F32), pltpu.VMEM((blocks,), jnp.int32), pltpu.VMEM((npairs,), jnp.int32),
            pltpu.VMEM((npairs,), jnp.int32), rows16, rows32, rows32,
            pltpu.SemaphoreType.DMA((len(CHUNK_STARTS),)), pltpu.SemaphoreType.DMA((4,)),
        ],
        (weights, right_side, block_fill, pair_home, pair_far, pair_count),
        in_hbm=range(5),
        in_smem=(5,),
    )
    held = pltpu.with_memory_space_constraint(held, pltpu.VMEM)
    flipped, token, put_home, pick_far = call(
        flip_kernel,
        [pltpu.VMEM(weights.shape, BF16), shape(8, tile),
         shape(blocks, npairs, dtype=BF16), shape(npairs, 9 * blocks, dtype=BF16)],
        [],
        (held, routes),
        cost=pl.CostEstimate(flops=0, bytes_accessed=weights.size * 6, transcendentals=0),
    )
    flipped = pltpu.with_memory_space_constraint(flipped, pltpu.VMEM)
    near, far_total, far_diag = exchanged(up, down, middle, middle_diag, token)
    v0 = right_side
    v1, diag, up, down, middle = call(
        second_kernel,
        [own_shape, own_shape, slabs(4), slabs(4), middle_shape],
        [rows16, rows32, rows32],
        (held, flipped, near, pick_far, put_home, pick_home, put_far, far_total, far_diag, v0, live, compress),
    )
    near, far_total = exchanged(up, down, middle)
    v2, up, down, middle = call(
        third_kernel,
        [own_shape, slabs(4), slabs(4), middle_shape],
        [rows16, rows32],
        (held, flipped, near, pick_far, put_home, pick_home, put_far, far_total, v1, live, diag),
    )
    near, far_total = exchanged(up, down, middle)
    image, dots = call(
        last_kernel,
        [own_shape, shape(size_first * size_second, tile)],
        [rows16, rows32],
        (flipped, near, pick_far, put_home, far_total, v0, v1, v2, live, diag),
    )
    dots = lax.all_to_all(dots, BOTH, 0, 0, tiled=True)
    return tuple(call(finish_kernel, [own_shape, own_shape], [], (dots, v0, v1, v2, image)))


def solution(mesh):
    return jax.shard_map(
        on_device,
        mesh=mesh,
        in_specs=(
            P(BOTH, None),
            P(BOTH, None),
            P(BOTH),
            P(BOTH),
            P(BOTH),
            P(BOTH),
            P(BOTH, None, None),
        ),
        out_specs=(P(BOTH, None), P(BOTH, None)),
        check_vma=False,
    )
```

```python
import jax
import jax.numpy as jnp
from jax import lax
from jax.experimental import pallas as pl
from jax.experimental.pallas import tpu as pltpu
from jax.sharding import PartitionSpec as P

SHIFT = 4.0
COMPRESS_MIN = 0.5
GROUP = 16
CHUNK_STARTS = (0, 256)
F32 = jnp.float32
BF16 = jnp.bfloat16
BOTH = ("gx", "gy")


def dot_rows(a, b):
    return lax.dot_general(a, b, (((1,), (0,)), ((), ())), preferred_element_type=F32)


def placed(onehot, terms):
    high = terms.astype(BF16)
    low = (terms - high.astype(F32)).astype(BF16)
    both = dot_rows(onehot, jnp.concatenate([high, low], axis=1))
    return both[:, :128] + both[:, 128:]


def pair_products(weights, vectors, out, sums, aside=0, arrive=None):
    sublane = lax.broadcasted_iota(jnp.int32, (8, 128), 0)
    zero = jnp.zeros((8, 128), F32)
    columns = vectors[...].astype(F32).T if aside else None

    def group(base):
        rows = pl.ds(base, GROUP)
        left = vectors[rows, :]
        if sums is not None:
            left = jnp.concatenate([left, jnp.ones((GROUP, 128), BF16)])
        results = [[zero, zero], [zero, zero]]

        def put(kind, pair, value):
            half = pair // 8
            results[kind][half] = jnp.where(sublane == pair % 8, value, results[kind][half])

        for pair in range(0, GROUP - aside, 2):
            product = dot_rows(left, jnp.concatenate([weights[base + pair], weights[base + pair + 1]], axis=1))
            for which in range(2):
                lanes = slice(128 * which, 128 * which + 128)
                for kind in range(1 if sums is None else 2):
                    start = GROUP * kind + (pair + which) // 8 * 8
                    put(kind, pair + which, product[start : start + 8, lanes])
        for pair in range(GROUP - aside, GROUP):
            tile = weights[base + pair].astype(F32)
            put(0, pair, jnp.sum(tile * columns[:, base + pair : base + pair + 1], axis=0, keepdims=True))
            if sums is not None:
                put(1, pair, jnp.sum(tile, axis=0, keepdims=True))
        out[rows, :] = jnp.concatenate(results[0])
        if sums is not None:
            sums[rows, :] = jnp.concatenate(results[1])

    for base in range(0, weights.shape[0], GROUP):
        if arrive is not None:
            arrive(base)
        group(base)


def send_terms(terms, up, down, middle, first):
    blocks = up.shape[1]
    for second in range(3):
        for target, slot in ((down, 0), (up, 2)):
            row = (3 * second + slot) * blocks
            target[first + second] = terms[row : row + blocks].astype(BF16)
        row = (3 * second + 1) * blocks
        middle[second] = terms[row : row + blocks]


def spread_down(row, count):
    return jnp.broadcast_to(row.astype(F32), (count, row.shape[1])).T


def start_kernel(weights, v_hbm, fill_hbm, home_hbm, far_hbm, count,
                 held, up, down, middle, middle_diag, live, pick_home, put_home, pick_far, put_far,
                 v, fill, home, far, vectors, products, sums, arrived, ready):
    blocks, tile = v.shape
    npairs = weights.shape[0]
    small = [
        pltpu.make_async_copy(source, target, ready.at[index])
        for index, (source, target) in enumerate(
            ((fill_hbm, fill), (v_hbm, v), (home_hbm, home), (far_hbm, far))
        )
    ]

    def copy(index):
        first, last = (*CHUNK_STARTS, npairs)[index : index + 2]
        part = pl.ds(first, last - first)
        return pltpu.make_async_copy(weights.at[part], held.at[part], arrived.at[index])

    for each in small:
        each.start()
    for index in range(len(CHUNK_STARTS)):
        copy(index).start()
    for each in small:
        each.wait()
    lane = lax.broadcasted_iota(jnp.int32, (blocks, tile), 1)
    mask = jnp.where(lane.astype(F32) < spread_down(fill[...].reshape(1, blocks), tile), 1.0, 0.0)
    live[...] = mask
    q = (mask * v[...]).astype(BF16)
    up[0] = q
    down[0] = q

    first_index, second_index = lax.axis_index("gx"), lax.axis_index("gy")
    size_second = lax.axis_size("gy")
    kept = lax.broadcasted_iota(jnp.int32, (1, npairs), 1) < count[0]
    far_block = far[...].reshape(1, npairs)
    far_device = lax.div(far_block, blocks)

    def slot_of(there, here):
        partner = here + 1 - 2 * lax.rem(here, 2)
        return jnp.where(there == here, 1, jnp.where(there == partner, 0, 2))

    slot_first = slot_of(lax.div(far_device, size_second), first_index)
    slot_second = slot_of(lax.rem(far_device, size_second), second_index)
    far_row = jnp.where(kept, (slot_second * 3 + slot_first) * blocks + lax.rem(far_block, blocks), -1)
    home_row = home[...].reshape(1, npairs) - (first_index * size_second + second_index) * blocks
    home_row = jnp.where(kept, home_row, -1)
    across = lax.broadcasted_iota(jnp.int32, (npairs, blocks), 1).astype(F32)
    along = lax.broadcasted_iota(jnp.int32, (blocks, npairs), 0)

    def mark(same):
        return jnp.where(same, 1.0, 0.0).astype(BF16)

    pick_home[...] = mark(across == spread_down(home_row, blocks))
    vectors[...] = dot_rows(pick_home[...], q).astype(BF16)
    put_home[...] = mark(along == home_row)
    far_column = spread_down(far_row, blocks)
    for slot in range(9):
        part = slice(slot * blocks, slot * blocks + blocks)
        pick_far[:, part] = mark(across + float(slot * blocks) == far_column)
        put_far[part, :] = mark(along + slot * blocks == far_row)


    def arrive(base):
        if base in CHUNK_STARTS:
            copy(CHUNK_STARTS.index(base)).wait()

    pair_products(held, vectors, products, sums, 2, arrive)
    both = jnp.concatenate([products[...].astype(BF16), sums[...].astype(BF16)], axis=1)
    both = dot_rows(put_far[...], both)
    send_terms(both[:, :tile], up, down, middle, 1)
    send_terms(both[:, tile:], up, down, middle_diag, 4)


def flip_kernel(weights, flipped, token):
    step = 16
    token[...] = jnp.zeros_like(token)

    def some(index, carry):
        for inner in range(step):
            flipped[index * step + inner] = weights[index * step + inner].T
        return carry

    lax.fori_loop(0, weights.shape[0] // step, some, 0)


def toward_home(flipped, near, pick_far, put_home, vectors, products, sums):
    vectors[...] = dot_rows(pick_far[...], near[...]).astype(BF16)
    pair_products(flipped, vectors, products, sums, 4 if sums is None else 2)
    return placed(put_home[...], products[...])


def away_next(weights, v, live, pick_home, put_far, up, down, middle, vectors, products):
    q = (live * v).astype(BF16)
    up[0] = q
    down[0] = q
    vectors[...] = dot_rows(pick_home[...], q).astype(BF16)
    pair_products(weights, vectors, products, None, 4)
    send_terms(dot_rows(put_far[...], products[...].astype(BF16)), up, down, middle, 1)


def second_kernel(weights, flipped, near, pick_far, put_home, pick_home, put_far, far_total, far_diag, v, live, compress,
                  after, diag_out, up, down, middle, vectors, products, sums):
    total = toward_home(flipped, near, pick_far, put_home, vectors, products, sums) + far_total[...]
    mask = live[...]
    diag = compress[...] + mask * (placed(put_home[...], sums[...]) + far_diag[...])
    diag_out[...] = diag
    result = (diag - SHIFT) * v[...] - mask * total
    after[...] = result
    away_next(weights, result, mask, pick_home, put_far, up, down, middle, vectors, products)


def third_kernel(weights, flipped, near, pick_far, put_home, pick_home, put_far, far_total, v, live, diag,
                 after, up, down, middle, vectors, products):
    total = toward_home(flipped, near, pick_far, put_home, vectors, products, None) + far_total[...]
    mask = live[...]
    result = (diag[...] - SHIFT) * v[...] - mask * total
    after[...] = result
    away_next(weights, result, mask, pick_home, put_far, up, down, middle, vectors, products)


def last_kernel(flipped, near, pick_far, put_home, far_total, v0, v1, v2, live, diag, image, dots, vectors, products):
    sums, mask = far_total[...], live[...]
    total = toward_home(flipped, near, pick_far, put_home, vectors, products, None) + sums
    a, b, c = v0[...], v1[...], v2[...]
    scaled = diag[...] * c
    image[...] = scaled - mask * total
    energy = c * (scaled - 2.0 * mask * sums)
    lane = lax.broadcasted_iota(jnp.int32, (1, 128), 1)
    row = jnp.zeros((1, 128), F32)
    for index, product in enumerate((a * a, a * b, a * c, b * b, b * c, c * c, energy)):
        result = jnp.sum(jnp.sum(product, axis=0, keepdims=True), axis=1, keepdims=True)
        row = jnp.where(lane == index, result, row)
    dots[...] = jnp.broadcast_to(row, dots.shape)


def finish_kernel(dots, v0, v1, v2, a2, solution_field, residual):
    row = jnp.sum(dots[...], axis=0, keepdims=True)
    lane = lax.broadcasted_iota(jnp.int32, row.shape, 1)

    def entry(index):
        return jnp.sum(jnp.where(lane == index, row, 0.0), axis=1, keepdims=True)

    g00, g01, g02, g11, g12, g22, m22 = (entry(index) for index in range(7))
    gram = ((g00, g01, g02), (g01, g11, g12), (g02, g12, g22))
    m00 = g01 + SHIFT * g00
    m01 = g11 + SHIFT * g01
    m11 = g12 + SHIFT * g11
    m02 = g12 + SHIFT * g02
    m12 = g22 + SHIFT * g12
    energies = ((m00, m01, m02), (m01, m11, m12), (m02, m12, m22))

    def form(matrix, p):
        return sum(p[i] * p[j] * matrix[i][j] for i in range(len(p)) for j in range(len(p)))

    def step_size(norm, p):
        floor = jnp.maximum(COMPRESS_MIN * norm, 1e-30)
        return norm / jnp.maximum(form(energies, p), floor)

    def moved(r, alpha, p):
        image = [SHIFT * p[i] + (p[i - 1] if i else 0.0) for i in range(len(p))] + [p[-1]]
        return [(r[i] if i < len(r) else 0.0) - alpha * image[i] for i in range(len(image))]

    def turned(r, beta, p):
        return [r[i] + beta * p[i] if i < len(p) else r[i] for i in range(len(r))]

    def norm_of(r):
        return jnp.maximum(form(gram, r), 0.0)

    one = jnp.ones_like(g00)
    p0 = [one]
    alpha0 = step_size(g00, p0)
    r1 = moved([one], alpha0, p0)
    n1 = norm_of(r1)
    p1 = turned(r1, n1 / jnp.maximum(g00, 1e-30), p0)
    alpha1 = step_size(n1, p1)
    r2 = moved(r1, alpha1, p1)
    n2 = norm_of(r2)
    p2 = turned(r2, n2 / jnp.maximum(n1, 1e-30), p1)
    alpha2 = step_size(n2, p2)
    x = [alpha0 * p0[0] + alpha1 * p1[0] + alpha2 * p2[0], alpha1 * p1[1] + alpha2 * p2[1], alpha2 * p2[2]]
    images = [SHIFT * p2[0], p2[0] + SHIFT * p2[1], p2[1]]
    r = [r2[i] - alpha2 * images[i] for i in range(3)]
    a, b, c = v0[...], v1[...], v2[...]
    solution_field[...] = x[0] * a + x[1] * b + x[2] * c
    residual[...] = r[0] * a + r[1] * b + r[2] * c - (alpha2 * p2[2]) * a2[...]


def swapped(value, axis, offset):
    count = lax.axis_size(axis)
    pairs = [(place, (((place + offset) ^ 1) - offset) % count) for place in range(count)]
    return lax.ppermute(value, axis, pairs)


def call(kernel, outs, scratch, args, in_hbm=(), in_smem=(), cost=None):
    args = [pltpu.with_memory_space_constraint(x, pltpu.HBM) if i in in_hbm else x for i, x in enumerate(args)]
    spaces = [pltpu.HBM if i in in_hbm else pltpu.SMEM if i in in_smem else pltpu.VMEM for i in range(len(args))]
    vmem = pl.BlockSpec(memory_space=pltpu.VMEM)
    return pl.pallas_call(
        kernel,
        out_shape=outs,
        in_specs=[pl.BlockSpec(memory_space=space) for space in spaces],
        out_specs=[vmem] * len(outs),
        scratch_shapes=scratch,
        cost_estimate=cost,
        compiler_params=pltpu.CompilerParams(vmem_limit_bytes=12 * 2**20),
    )(*args)


def exchanged(up, down, middle, middle_diag=None, token=None):
    low, high = swapped(down, "gx", 0), swapped(up, "gx", 1)
    column = jnp.stack([low[0], up[0], high[0]])

    def summed(second, first, own):
        return own[second] + low[first + second].astype(F32) + high[first + second].astype(F32)

    kinds = [(1, middle)] if middle_diag is None else [(1, middle), (4, middle_diag)]

    def message(second):
        sums = [summed(second, first, own) for first, own in kinds]
        if token is not None:
            sums = [each + token[:1] for each in sums]
        sums = [each.astype(BF16)[None] for each in sums]
        return jnp.concatenate([column, *sums])

    from_low, from_high = swapped(message(0), "gy", 0), swapped(message(2), "gy", 1)
    near = jnp.concatenate([from_low[:3], column, from_high[:3]])
    near = near.reshape(-1, near.shape[-1])
    totals = [
        summed(1, first, own) + from_low[3 + kind].astype(F32) + from_high[3 + kind].astype(F32)
        for kind, (first, own) in enumerate(kinds)
    ]
    return near, *totals


def on_device(right_side, compress, block_fill, pair_home, pair_far, pair_count, weights):
    blocks, tile = right_side.shape
    npairs = weights.shape[0]
    size_first, size_second = lax.axis_size("gx"), lax.axis_size("gy")

    def shape(*dims, dtype=F32):
        return jax.ShapeDtypeStruct(dims, dtype)

    own_shape = shape(blocks, tile)
    middle_shape = shape(3, blocks, tile)
    rows16, rows32 = pltpu.VMEM((npairs, tile), BF16), pltpu.VMEM((npairs, tile), F32)

    def slabs(count):
        return shape(count, blocks, tile, dtype=BF16)

    pick = shape(npairs, blocks, dtype=BF16), shape(blocks, npairs, dtype=BF16)
    pick += shape(npairs, 9 * blocks, dtype=BF16), shape(9 * blocks, npairs, dtype=BF16)
    held, up, down, middle, middle_diag, live, pick_home, put_home, pick_far, put_far = call(
        start_kernel,
        [pltpu.VMEM(weights.shape, BF16), slabs(7), slabs(7), middle_shape, middle_shape, own_shape, *pick],
        [
            pltpu.VMEM((blocks, tile), F32), pltpu.VMEM((blocks,), jnp.int32), pltpu.VMEM((npairs,), jnp.int32),
            pltpu.VMEM((npairs,), jnp.int32), rows16, rows32, rows32,
            pltpu.SemaphoreType.DMA((len(CHUNK_STARTS),)), pltpu.SemaphoreType.DMA((4,)),
        ],
        (weights, right_side, block_fill, pair_home, pair_far, pair_count),
        in_hbm=range(5),
        in_smem=(5,),
    )
    held = pltpu.with_memory_space_constraint(held, pltpu.VMEM)
    flipped, token = call(
        flip_kernel,
        [pltpu.VMEM(weights.shape, BF16), shape(8, tile)],
        [],
        (held,),
        cost=pl.CostEstimate(flops=0, bytes_accessed=weights.size * 6, transcendentals=0),
    )
    flipped = pltpu.with_memory_space_constraint(flipped, pltpu.VMEM)
    near, far_total, far_diag = exchanged(up, down, middle, middle_diag, token)
    v0 = right_side
    v1, diag, up, down, middle = call(
        second_kernel,
        [own_shape, own_shape, slabs(4), slabs(4), middle_shape],
        [rows16, rows32, rows32],
        (held, flipped, near, pick_far, put_home, pick_home, put_far, far_total, far_diag, v0, live, compress),
    )
    near, far_total = exchanged(up, down, middle)
    v2, up, down, middle = call(
        third_kernel,
        [own_shape, slabs(4), slabs(4), middle_shape],
        [rows16, rows32],
        (held, flipped, near, pick_far, put_home, pick_home, put_far, far_total, v1, live, diag),
    )
    near, far_total = exchanged(up, down, middle)
    image, dots = call(
        last_kernel,
        [own_shape, shape(size_first * size_second, tile)],
        [rows16, rows32],
        (flipped, near, pick_far, put_home, far_total, v0, v1, v2, live, diag),
    )
    dots = lax.all_to_all(dots, BOTH, 0, 0, tiled=True)
    return tuple(call(finish_kernel, [own_shape, own_shape], [], (dots, v0, v1, v2, image)))


def solution(mesh):
    return jax.shard_map(
        on_device,
        mesh=mesh,
        in_specs=(
            P(BOTH, None),
            P(BOTH, None),
            P(BOTH),
            P(BOTH),
            P(BOTH),
            P(BOTH),
            P(BOTH, None, None),
        ),
        out_specs=(P(BOTH, None), P(BOTH, None)),
        check_vma=False,
    )
```
